128 devices in a mesh: brick: 8 (over x, core), group: 16 (over y, z).
Axes of the slice: x: 4, y: 4, z: 4, core: 2. Of those that a mesh axis runs over, the one named last changes fastest.
Arguments:
- right_side: float32 [64, 16384], P(None, ('brick', 'group')), may hold values from -6 to 6
- fine_diag: bfloat16 [64, 64, 16384], P(None, None, ('brick', 'group'))
- fine_off: bfloat16 [6, 64, 64, 16384], P(None, None, None, ('brick', 'group')), may hold values from -0.1875 to 0.1875
- fine_inv: bfloat16 [64, 64, 16384], P(None, None, ('brick', 'group'))
- fine_columns: int32 [6, 16384], P(None, ('brick', 'group')), may hold values from -32 to 16415, as said below
- aggregate: int32 [16384], P(('brick', 'group')), may hold values from 0 to 15, as said below
- coarse_diag: bfloat16 [64, 64, 2048], P(None, None, ('brick', 'group'))
- coarse_off: bfloat16 [8, 64, 64, 2048], P(None, None, None, ('brick', 'group')), may hold values from -0.125 to 0.125
- coarse_inv: bfloat16 [64, 64, 2048], P(None, None, ('brick', 'group'))
- coarse_columns: int32 [8, 2048], P(None, ('brick', 'group')), may hold values from 0 to 2047, as said below
Outputs:
- solution: float32 [64, 16384], P(None, ('brick', 'group'))
The draws below stay inside these ranges and needn't reach their ends.
Inputs may be any that keep to these rules, and one draw needn't show every extreme that they name: `fine_columns`: each fine block row has exactly 6 off-diagonal blocks, whose columns lie within 32 block rows of their row. Within each device's 128 fine block rows aggregate never falls and takes every value; each aggregate is a run of consecutive rows. `coarse_columns`: each coarse block row has exactly 8 off-diagonal blocks, whose columns lie within 16 coarse rows of their row.
All inputs are finite; a program needn't handle non-finite values.
Results may differ from the reference program's by a relative error of at most 0.0003.
Values sent between devices are 32-bit elements; how exact they have to be, the bound alone decides.
No kernel may reach another device: no remote copies, remote signals or barrier semaphores. Data moves between devices by JAX's collectives and lax.ppermute only.
A program may use at most 64 MiB of HBM per device.

```python
import math
import jax
import jax.numpy as jnp

BS = 64
NNZ = 6
NNZC = 8
RB = 128
RATIO = 8
SWEEPS = 2
CSWEEPS = 4
CYCLES = 2
HB = 32
AGG = 16
NB = 16384
NC = 2048


def dominant(key, count, center, spread):
    noise = jax.random.normal(key, (BS, BS, count), jnp.float32) * (spread / math.sqrt(BS))
    return jnp.eye(BS, dtype=jnp.float32)[:, :, None] * center + noise


def draw_fine_diag(key, part):
    return dominant(key, NB, 2.0, 0.64).astype(jnp.bfloat16)


def draw_fine_inv(key, part):
    return dominant(key, NB, 0.5, 0.16).astype(jnp.bfloat16)


def draw_coarse_diag(key, part):
    return dominant(key, NC, 2.0, 0.64).astype(jnp.bfloat16)


def draw_coarse_inv(key, part):
    return dominant(key, NC, 0.5, 0.16).astype(jnp.bfloat16)


def draw_fine_columns(key, part):
    first, second = jax.random.split(key)
    reach = jax.random.randint(first, (NNZ, NB), 1, HB + 1)
    signs = 2 * jax.random.randint(second, (NNZ, NB), 0, 2) - 1
    columns = jnp.arange(NB, dtype=jnp.int32)[None, :] + signs * reach
    columns = columns.at[0, 0].set(0 - HB).at[NNZ - 1, NB - 1].set(NB - 1 + HB)
    return columns.astype(jnp.int32)


def draw_aggregate(key, part):
    count = NB // RB
    jitter = jax.random.randint(key, (count, AGG), 1 - RATIO // 2, RATIO // 2)
    jitter = jitter.at[:, 0].set(0)
    starts = jnp.arange(AGG, dtype=jnp.int32)[None, :] * RATIO + jitter
    places = jnp.arange(RB, dtype=jnp.int32)
    values = jnp.sum((starts[:, :, None] <= places[None, None, :]).astype(jnp.int32), axis=1) - 1
    return values.reshape(NB).astype(jnp.int32)


def draw_coarse_columns(key, part):
    first, second = jax.random.split(key)
    reach = jax.random.randint(first, (NNZC, NC), 1, AGG + 1)
    signs = 2 * jax.random.randint(second, (NNZC, NC), 0, 2) - 1
    rows = jnp.arange(NC, dtype=jnp.int32)[None, :]
    columns = rows + signs * reach
    columns = jnp.where(columns < 0, rows + reach, columns)
    columns = jnp.where(columns > NC - 1, rows - reach, columns)
    columns = columns.at[0, 1].set(0).at[NNZC - 1, NC - 2].set(NC - 1)
    return columns.astype(jnp.int32)


def block_levels(rng, dims, cuts, low, high):
    gain = 1.0
    for position, parts in cuts:
        steps = jax.random.uniform(jax.random.fold_in(jax.random.fold_in(rng, 6), position), (parts,), jnp.float32, low / len(cuts), high / len(cuts))
        gain = gain * jnp.repeat(jnp.exp(steps), dims[position] // parts).reshape((-1,) + (1,) * (len(dims) - 1 - position))
    return gain


def normal_values(own_key, dims, deviation, most, pieces=(), held_as=jnp.bfloat16):
    entries = deviation * jax.random.normal(own_key, dims, jnp.float32)
    if pieces:
        entries = entries * block_levels(own_key, dims, pieces, -0.22, 0.18)
    return jnp.clip(entries, -most, most).astype(held_as)


def setup_inputs(seed: int = 0) -> dict:
    streams_of = jax.random.split(jax.random.key(seed), 11)
    right_side = normal_values(streams_of[0], (BS, NB), 1.0, 6.0, ((1, 128),), jnp.float32)
    fine_diag = draw_fine_diag(jax.random.fold_in(streams_of[10], 71), 0)
    fine_off = normal_values(streams_of[2], (NNZ, BS, BS, NB), (16 * BS) ** -0.5, 0.1875, ((3, 128),))
    fine_inv = draw_fine_inv(jax.random.fold_in(streams_of[10], 71), 0)
    fine_columns = draw_fine_columns(jax.random.fold_in(streams_of[10], 71), 0)
    aggregate = draw_aggregate(jax.random.fold_in(streams_of[10], 71), 0)
    coarse_diag = draw_coarse_diag(jax.random.fold_in(streams_of[10], 71), 0)
    coarse_off = normal_values(streams_of[7], (NNZC, BS, BS, NC), (40 * BS) ** -0.5, 0.125, ((3, 128),))
    coarse_inv = draw_coarse_inv(jax.random.fold_in(streams_of[10], 71), 0)
    coarse_columns = draw_coarse_columns(jax.random.fold_in(streams_of[10], 71), 0)
    return dict(right_side=right_side, fine_diag=fine_diag, fine_off=fine_off, fine_inv=fine_inv, fine_columns=fine_columns, aggregate=aggregate, coarse_diag=coarse_diag, coarse_off=coarse_off, coarse_inv=coarse_inv, coarse_columns=coarse_columns)


damping = 0.7


def apply_blocks(blocks, field):
    return jnp.sum(blocks.astype(jnp.float32) * field[None, :, :], axis=1)


def fine_product(field, fine_diag, fine_off, fine_columns):
    padded = jnp.pad(field, ((0, 0), (HB, HB)))
    total = apply_blocks(fine_diag, field)
    for slot in range(NNZ):
        picked = padded[:, (fine_columns[slot] + HB).astype(jnp.int32)]
        total = total + apply_blocks(fine_off[slot], picked)
    return total


def coarse_product(field, coarse_diag, coarse_off, coarse_columns):
    total = apply_blocks(coarse_diag, field)
    for slot in range(NNZC):
        total = total + apply_blocks(coarse_off[slot], field[:, coarse_columns[slot]])
    return total


def reference(right_side, fine_diag, fine_off, fine_inv, fine_columns, aggregate, coarse_diag, coarse_off, coarse_inv, coarse_columns):
    device = jnp.arange(NB, dtype=jnp.int32) // RB
    target = (device * AGG + aggregate).astype(jnp.int32)

    def sweep(solution):
        residual = right_side - fine_product(solution, fine_diag, fine_off, fine_columns)
        return solution + damping * apply_blocks(fine_inv, residual)

    solution = jnp.zeros((BS, NB), jnp.float32)
    for cycle in range(CYCLES):
        for step in range(SWEEPS):
            solution = sweep(solution)
        residual = right_side - fine_product(solution, fine_diag, fine_off, fine_columns)
        coarse_rhs = jax.ops.segment_sum(residual.T, target, num_segments=NC).T
        correction = jnp.zeros((BS, NC), jnp.float32)
        for step in range(CSWEEPS):
            coarse_res = coarse_rhs - coarse_product(correction, coarse_diag, coarse_off, coarse_columns)
            correction = correction + damping * apply_blocks(coarse_inv, coarse_res)
        solution = solution + correction[:, target]
        for step in range(SWEEPS):
            solution = sweep(solution)
    return solution
```

```python
import jax
import jax.numpy as jnp
from jax import lax
from jax.experimental import pallas as pl
from jax.experimental.pallas import tpu as pltpu
from jax.sharding import PartitionSpec as P

SWEEPS = 2
CSWEEPS = 4
CYCLES = 2
AXES = ("brick", "group")
LINE = 4

damping = 0.7
LANES = 128
F32 = jnp.float32


def routes(count):
    lines = count // LINE
    up, down, cross = [], [], []
    for i in range(count):
        base = i - i % LINE
        up.append((i, base + (i + 1) % LINE))
        down.append((i, base + (i - 1) % LINE))
    for k in range(lines - 1):
        a, b = LINE * k + LINE - 1, LINE * k + LINE
        cross += [(a, b), (b, a)]
    for k in range(1, lines - 1):
        a, b = LINE * k + 1, LINE * k + 2
        cross += [(a, b), (b, a)]
    last = count - 1
    cross += [(0, 1), (1, 2), (2, 0), (last - 2, last - 1), (last - 1, last), (last, last - 2)]
    return up, down, cross


def exchange(field, ways):
    return [lax.ppermute(field, AXES, way) for way in ways]


def iota(shape, dim):
    return lax.broadcasted_iota(jnp.int32, shape, dim)


def fold_sublanes(parts):
    rows = iota(parts[0].shape, 0)
    shift = 4
    while shift:
        low = (rows & shift) == 0
        parts = [
            jnp.where(low, a, b) + pltpu.roll(jnp.where(low, b, a), 4 if shift == 4 else (8 - shift), 0)
            if shift == 4
            else fold_pair(a, b, low, shift, 0)
            for a, b in zip(parts[:shift], parts[shift:])
        ]
        shift //= 2
    return parts[0]


def fold_pair(a, b, low, shift, axis):
    size = a.shape[axis]
    own = jnp.where(low, a, b)
    other = jnp.where(low, b, a)
    return own + jnp.where(
        low, pltpu.roll(other, size - shift, axis), pltpu.roll(other, shift, axis)
    )


def fold_lanes(parts):
    lanes = iota(parts[0].shape, 1)
    shift, half = 64, 4
    while half:
        low = (lanes & shift) == 0
        if shift == 64:
            parts = [
                jnp.where(low, a, b) + pltpu.roll(jnp.where(low, b, a), 64, 1)
                for a, b in zip(parts[:half], parts[half:])
            ]
        else:
            parts = [fold_pair(a, b, low, shift, 1) for a, b in zip(parts[:half], parts[half:])]
        shift //= 2
        half //= 2
    return parts[0]


def take_lanes(field, places):
    return jnp.take_along_axis(field, places, axis=1, mode="promise_in_bounds")


def apply_fine(blocks, fields, a_block):
    acc = jnp.zeros((8, 8, LANES), F32)
    for slot in range(blocks.shape[0]):
        for g in range(4):
            piece = blocks[slot, pl.ds(pl.multiple_of(a_block * 8, 8), 8), 16 * g : 16 * g + 16, :].astype(F32)
            v = fields[slot, 16 * g : 16 * g + 16, :]
            acc = acc + piece[:, :8] * v[None, :8]
            acc = acc + piece[:, 8:] * v[None, 8:]
    return fold_sublanes([acc[i] for i in range(8)])


def neighbours(flags, up, down, cross):
    left = jnp.where(flags[0] == 1, cross, up)
    right = jnp.where(flags[1] == 1, cross, down)
    left = jnp.where(flags[2] == 1, 0.0, left)
    right = jnp.where(flags[3] == 1, 0.0, right)
    return left, right


def gather_fine(flags, columns, x_ref, up, down, cross, fields):
    lanes = iota((8, LANES), 1)
    slots = columns.shape[0]
    places = [jnp.broadcast_to(columns[s : s + 1, :], (8, LANES)) for s in range(slots)]
    lane_of = [p & (LANES - 1) for p in places]
    own = [(p >= 0) & (p < LANES) for p in places]
    for g in range(8):
        part = slice(8 * g, 8 * g + 8)
        left, right = neighbours(flags, up[part, :], down[part, :], cross[part, :])
        rim = jnp.where(lanes < LANES // 2, right, left)
        x = x_ref[part, :]
        fields[0, part, :] = x
        for s in range(slots):
            fields[s + 1, part, :] = jnp.where(
                own[s], take_lanes(x, lane_of[s]), take_lanes(rim, lane_of[s])
            )


def residual_into(res, rhs, diag, off, fields):
    def body(ab, carry):
        acc = jnp.zeros((8, 8, LANES), F32)
        rows = pl.ds(pl.multiple_of(ab * 8, 8), 8)
        for slot in range(fields.shape[0]):
            for g in range(4):
                src = diag[rows, 16 * g : 16 * g + 16, :] if slot == 0 else off[slot - 1, rows, 16 * g : 16 * g + 16, :]
                piece = src.astype(F32)
                v = fields[slot, 16 * g : 16 * g + 16, :]
                acc = acc + piece[:, :8] * v[None, :8]
                acc = acc + piece[:, 8:] * v[None, 8:]
        res[rows, :] = rhs[rows, :] - fold_sublanes([acc[i] for i in range(8)])
        return carry

    lax.fori_loop(0, 8, body, 0)


def smooth_into(out, x, inv, res):
    def body(ab, carry):
        acc = jnp.zeros((8, 8, LANES), F32)
        rows = pl.ds(pl.multiple_of(ab * 8, 8), 8)
        for g in range(4):
            piece = inv[rows, 16 * g : 16 * g + 16, :].astype(F32)
            v = res[16 * g : 16 * g + 16, :]
            acc = acc + piece[:, :8] * v[None, :8]
            acc = acc + piece[:, 8:] * v[None, 8:]
        step = damping * fold_sublanes([acc[i] for i in range(8)])
        out[rows, :] = step if x is None else x[rows, :] + step
        return carry

    lax.fori_loop(0, 8, body, 0)


def first_kernel(inv, rhs, out):
    smooth_into(out, None, inv, rhs)


def sweep_kernel(flags, columns, diag, off, inv, rhs, x, up, down, cross, out, fields, res):
    gather_fine(flags, columns, x, up, down, cross, fields)
    residual_into(res, rhs, diag, off, fields)
    smooth_into(out, x, inv, res)


def pack_rows(full):
    group = iota((8, LANES), 1) // 16
    out = full[0:8, :]
    for g in range(1, 8):
        out = jnp.where(group == g, full[8 * g : 8 * g + 8, :], out)
    return out


def small_apply(blocks, packed, extra=None, fields=None):
    parts = []
    for ab in range(8):
        acc = blocks[8 * ab : 8 * ab + 8] * packed[None]
        if extra is not None:
            for g in range(8):
                acc = acc + extra[8 * ab : 8 * ab + 8, 8 * g : 8 * g + 8, :] * fields[g][None]
        parts.append(fold_sublanes([acc[i] for i in range(8)]))
    return fold_lanes(parts)


def restrict_kernel(flags, columns, diag, off, rhs, x, up, down, cross, agg, cinv, coarse_rhs, out, fields, res):
    gather_fine(flags, columns, x, up, down, cross, fields)
    residual_into(res, rhs, diag, off, fields)
    r = res[...]
    hi = r.astype(jnp.bfloat16)
    rest = r - hi.astype(F32)
    mid = rest.astype(jnp.bfloat16)
    low = (rest - mid.astype(F32)).astype(jnp.bfloat16)
    parts = jnp.concatenate([hi, mid, low], axis=0)
    row_of = jnp.broadcast_to(agg[...], (LANES, LANES))
    select = jnp.where(row_of == (iota((LANES, LANES), 0) & 15), 1.0, 0.0).astype(jnp.bfloat16)
    sums = lax.dot_general(parts, select, (((1,), (1,)), ((), ())), preferred_element_type=F32)
    full = sums[0:64] + (sums[64:128] + sums[128:192])
    packed = pack_rows(full)
    coarse_rhs[...] = packed
    out[...] = damping * small_apply(cinv, packed)


def coarse_step(flags, columns, cdiag, coff, cinv, coarse_rhs, u, up, down, cross):
    left, right = neighbours(flags, up[...], down[...], cross[...])
    places = jnp.broadcast_to(columns[...], (8, LANES))
    inner = places & 15
    mine = u[...]
    fields = []
    for g in range(8):
        lane = inner + 16 * g
        fields.append(
            jnp.where(
                places < 0,
                take_lanes(left, lane),
                jnp.where(places < 16, take_lanes(mine, lane), take_lanes(right, lane)),
            )
        )
    total = small_apply(cdiag, mine, coff, fields)
    return mine + damping * small_apply(cinv, coarse_rhs[...] - total)


def coarse_kernel(flags, columns, cdiag, coff, cinv, coarse_rhs, u, up, down, cross, out):
    out[...] = coarse_step(flags, columns, cdiag, coff, cinv, coarse_rhs, u, up, down, cross)


def prolong_kernel(flags, columns, cdiag, coff, cinv, coarse_rhs, u, up, down, cross, agg, x, out):
    last = coarse_step(flags, columns, cdiag, coff, cinv, coarse_rhs, u, up, down, cross)
    lane = jnp.broadcast_to(agg[...], (8, LANES))
    for g in range(8):
        part = slice(8 * g, 8 * g + 8)
        out[part, :] = x[part, :] + take_lanes(last, lane + 16 * g)


def in_vmem(array):
    return pltpu.with_memory_space_constraint(array, pltpu.VMEM)


VM = pl.BlockSpec(memory_space=pltpu.VMEM)
SM = pl.BlockSpec(memory_space=pltpu.SMEM)


def call(kernel, outs, args, scratch=(), smem=False, flops=0, name=None):
    shapes = [pltpu.VMEM(shape, F32) for shape in outs]
    specs = [VM] * len(args)
    if smem:
        specs[0] = SM
    args = [a if (smem and i == 0) else in_vmem(a) for i, a in enumerate(args)]
    result = pl.pallas_call(
        kernel,
        out_shape=shapes if len(shapes) > 1 else shapes[0],
        in_specs=specs,
        out_specs=[VM] * len(shapes) if len(shapes) > 1 else VM,
        scratch_shapes=list(scratch),
        compiler_params=pltpu.CompilerParams(vmem_limit_bytes=4 * 1024 * 1024),
        name=name,
    )(*args)
    return result


def shards(
    right_side,
    fine_diag,
    fine_off,
    fine_inv,
    fine_columns,
    aggregate,
    coarse_diag,
    coarse_off,
    coarse_inv,
    coarse_columns,
):
    size, rows = right_side.shape
    slots = fine_off.shape[0]
    own_rows = coarse_diag.shape[2]
    cslots = coarse_off.shape[0]
    count = lax.axis_size(AXES)
    device = lax.axis_index(AXES)
    ways = routes(count)
    flags = jnp.stack(
        [
            device % LINE == 0,
            device % LINE == LINE - 1,
            device == 0,
            device == count - 1,
        ]
    ).astype(jnp.int32)
    columns = fine_columns - device * rows
    ccolumns = (coarse_columns - device * own_rows).reshape(1, cslots * own_rows)
    agg = aggregate.reshape(1, rows)
    coff = jnp.transpose(coarse_off, (1, 2, 0, 3)).reshape(size, size, cslots * own_rows).astype(F32)

    def packed_blocks(blocks):
        split = blocks.reshape(size, 8, 8, own_rows)
        return jnp.transpose(split, (0, 2, 1, 3)).reshape(size, 8, 8 * own_rows).astype(F32)

    cdiag = packed_blocks(coarse_diag)
    cinv = packed_blocks(coarse_inv)

    full = (size, rows)
    packed = (8, LANES)
    scratch = [pltpu.VMEM((slots + 1,) + full, F32), pltpu.VMEM(full, F32)]

    def sweep(x):
        return call(
            sweep_kernel,
            [full],
            [flags, columns, fine_diag, fine_off, fine_inv, right_side, x, *exchange(x, ways)],
            scratch,
            smem=True,
        )

    x = call(first_kernel, [full], [fine_inv, right_side])
    for cycle in range(CYCLES):
        for step in range(SWEEPS):
            if cycle or step:
                x = sweep(x)
        crhs, u = call(
            restrict_kernel,
            [packed, packed],
            [flags, columns, fine_diag, fine_off, right_side, x, *exchange(x, ways), agg, cinv],
            scratch,
            smem=True,
        )
        for step in range(1, CSWEEPS):
            base = [flags, ccolumns, cdiag, coff, cinv, crhs, u, *exchange(u, ways)]
            if step < CSWEEPS - 1:
                u = call(coarse_kernel, [packed], base, smem=True)
            else:
                x = call(prolong_kernel, [full], base + [agg, x], smem=True)
        for step in range(SWEEPS):
            x = sweep(x)
    return x


def solution(mesh):
    placed = (
        P(None, AXES),
        P(None, None, AXES),
        P(None, None, None, AXES),
        P(None, None, AXES),
        P(None, AXES),
        P(AXES),
        P(None, None, AXES),
        P(None, None, None, AXES),
        P(None, None, AXES),
        P(None, AXES),
    )
    return jax.shard_map(
        shards, mesh=mesh, in_specs=placed, out_specs=P(None, AXES), check_vma=False
    )
```

```python
import jax
import jax.numpy as jnp
from jax import lax
from jax.experimental import pallas as pl
from jax.experimental.pallas import tpu as pltpu
from jax.sharding import PartitionSpec as P

SWEEPS = 2
CSWEEPS = 4
CYCLES = 2
AXES = ("brick", "group")
LINE = 4

damping = 0.7
LANES = 128
F32 = jnp.float32


def routes(count):
    lines = count // LINE
    up, down, cross = [], [], []
    for i in range(count):
        base = i - i % LINE
        up.append((i, base + (i + 1) % LINE))
        down.append((i, base + (i - 1) % LINE))
    for k in range(lines - 1):
        a, b = LINE * k + LINE - 1, LINE * k + LINE
        cross += [(a, b), (b, a)]
    for k in range(1, lines - 1):
        a, b = LINE * k + 1, LINE * k + 2
        cross += [(a, b), (b, a)]
    last = count - 1
    cross += [(0, 1), (1, 2), (2, 0), (last - 2, last - 1), (last - 1, last), (last, last - 2)]
    return up, down, cross


def exchange(field, ways):
    up, down, cross = ways
    down = lax.ppermute(field, AXES, down)
    up = lax.ppermute(field, AXES, up)
    cross = lax.ppermute(field, AXES, cross)
    return up, down, cross


def iota(shape, dim):
    return lax.broadcasted_iota(jnp.int32, shape, dim)


def fold_sublanes(parts):
    rows = iota(parts[0].shape, 0)
    shift = 4
    while shift:
        low = (rows & shift) == 0
        parts = [
            jnp.where(low, a, b) + pltpu.roll(jnp.where(low, b, a), 4 if shift == 4 else (8 - shift), 0)
            if shift == 4
            else fold_pair(a, b, low, shift, 0)
            for a, b in zip(parts[:shift], parts[shift:])
        ]
        shift //= 2
    return parts[0]


def fold_pair(a, b, low, shift, axis):
    size = a.shape[axis]
    own = jnp.where(low, a, b)
    other = jnp.where(low, b, a)
    return own + jnp.where(
        low, pltpu.roll(other, size - shift, axis), pltpu.roll(other, shift, axis)
    )


def fold_lanes(parts):
    lanes = iota(parts[0].shape, 1)
    shift, half = 64, 4
    while half:
        low = (lanes & shift) == 0
        if shift == 64:
            parts = [
                jnp.where(low, a, b) + pltpu.roll(jnp.where(low, b, a), 64, 1)
                for a, b in zip(parts[:half], parts[half:])
            ]
        else:
            parts = [fold_pair(a, b, low, shift, 1) for a, b in zip(parts[:half], parts[half:])]
        shift //= 2
        half //= 2
    return parts[0]


def take_lanes(field, places):
    return jnp.take_along_axis(field, places, axis=1, mode="promise_in_bounds")


def neighbours(flags, up, down, cross):
    left = jnp.where(flags[0] == 1, cross, up)
    right = jnp.where(flags[1] == 1, cross, down)
    left = jnp.where(flags[2] == 1, 0.0, left)
    right = jnp.where(flags[3] == 1, 0.0, right)
    return left, right


def gather_fine(flags, columns, x_ref, up, down, cross, fields):
    lanes = iota((8, LANES), 1)
    slots = columns.shape[0]
    places = [jnp.broadcast_to(columns[s : s + 1, :], (8, LANES)) for s in range(slots)]
    lane_of = [p & (LANES - 1) for p in places]
    own = [(p >= 0) & (p < LANES) for p in places]
    for g in range(8):
        part = slice(8 * g, 8 * g + 8)
        left, right = neighbours(flags, up[part, :], down[part, :], cross[part, :])
        rim = jnp.where(lanes < LANES // 2, right, left)
        x = x_ref[part, :]
        fields[0, part, :] = x
        for s in range(slots):
            fields[s + 1, part, :] = jnp.where(
                own[s], take_lanes(x, lane_of[s]), take_lanes(rim, lane_of[s])
            )


def fold_rows(acc, block):
    return fold_sublanes([acc[8 * block + i] for i in range(8)])


def residual_into(res, rhs, diag, off, fields, acc):
    def body(ab, carry):
        rows = pl.ds(pl.multiple_of(ab * 8, 8), 8)
        total = jnp.zeros((8, 8, LANES), F32)
        for slot in range(fields.shape[0]):
            for g in range(8):
                part = slice(8 * g, 8 * g + 8)
                piece = diag[rows, part, :] if slot == 0 else off[slot - 1, rows, part, :]
                total = total + piece * fields[slot, part, :][None]
        acc[rows] = total
        return carry

    lax.fori_loop(0, 8, body, 0)
    for ab in range(8):
        rows = slice(8 * ab, 8 * ab + 8)
        res[rows, :] = rhs[rows, :] - fold_rows(acc, ab)


def smooth_into(out, x, inv, res):
    for ab in range(8):
        rows = slice(8 * ab, 8 * ab + 8)
        total = inv[rows, 0:8, :] * res[0:8, :][None]
        for g in range(1, 8):
            part = slice(8 * g, 8 * g + 8)
            total = total + inv[rows, part, :] * res[part, :][None]
        out[rows, :] = x[rows, :] + damping * fold_sublanes([total[i] for i in range(8)])


def first_kernel(inv, rhs, out, inv_out, rhs_out, held, rhs_sem, sems):
    copies = [
        pltpu.make_async_copy(inv.at[pl.ds(8 * k, 8)], held.at[pl.ds(8 * k, 8)], sems.at[k])
        for k in range(8)
    ]
    lead = pltpu.make_async_copy(rhs, rhs_out, rhs_sem)
    lead.start()
    for copy in copies:
        copy.start()
    lead.wait()
    for k in range(8):
        copies[k].wait()
        rows = slice(8 * k, 8 * k + 8)
        total = jnp.zeros((8, 8, LANES), F32)
        for g in range(4):
            piece = held[rows, 16 * g : 16 * g + 16, :].astype(F32)
            inv_out[rows, 16 * g : 16 * g + 16, :] = piece
            total = total + piece[:, :8] * rhs_out[16 * g : 16 * g + 8, :][None]
            total = total + piece[:, 8:] * rhs_out[16 * g + 8 : 16 * g + 16, :][None]
        out[rows, :] = damping * fold_sublanes([total[i] for i in range(8)])


def widen_kernel(diag, off, diag_out, off_out, held, sems):
    slots = off.shape[0]
    copies = [pltpu.make_async_copy(diag, held.at[0], sems.at[0])]
    for s in range(slots):
        copies.append(pltpu.make_async_copy(off.at[s], held.at[s + 1], sems.at[s + 1]))
    for copy in copies:
        copy.start()
    for s in range(slots + 1):
        copies[s].wait()

        def body(ab, carry):
            rows = pl.ds(pl.multiple_of(ab * 8, 8), 8)
            wide = held[s, rows].astype(F32)
            if s == 0:
                diag_out[rows] = wide
            else:
                off_out[s - 1, rows] = wide
            return carry

        lax.fori_loop(0, 8, body, 0)


def coarse_prep_kernel(diag, off, inv, diag_out, off_out, inv_out, diag_in, off_in, inv_in, sems):
    size = diag.shape[0]
    copies = [
        pltpu.make_async_copy(inv, inv_in, sems.at[0]),
        pltpu.make_async_copy(diag, diag_in, sems.at[1]),
        pltpu.make_async_copy(off, off_in, sems.at[2]),
    ]
    for copy in copies:
        copy.start()
    eye = jnp.where(iota((size, size), 0) == iota((size, size), 1), 1.0, 0.0).astype(jnp.bfloat16)

    def turned(block):
        return lax.dot_general(eye, block, (((1,), (1,)), ((), ())), preferred_element_type=F32)

    for copy, src, dst in ((copies[0], inv_in, inv_out), (copies[1], diag_in, diag_out)):
        copy.wait()
        for r in range(8):
            dst[r] = turned(jnp.concatenate([src[8 * h + r] for h in range(8)], axis=0))
    copies[2].wait()

    def body(a, carry):
        for k in range(4):
            block = jnp.concatenate([off_in[s, 4 * a + k] for s in range(off_in.shape[0])], axis=0)
            off_out[4 * a + k] = turned(block)
        return carry

    lax.fori_loop(0, size // 4, body, 0)


def sweep_kernel(flags, columns, diag, off, inv, rhs, x, up, down, cross, out, fields, res, acc):
    gather_fine(flags, columns, x, up, down, cross, fields)
    residual_into(res, rhs, diag, off, fields, acc)
    smooth_into(out, x, inv, res)


def pack_rows(full):
    group = iota((8, LANES), 1) // 16
    out = full[0:8, :]
    for g in range(1, 8):
        out = jnp.where(group == g, full[8 * g : 8 * g + 8, :], out)
    return out


def spread_rows(packed):
    lane = iota((8, LANES), 1) & 15
    return [take_lanes(packed, lane + 16 * h) for h in range(8)]


def small_apply(blocks, fields):
    parts = []
    for r in range(8):
        acc = blocks[r, 0:8, :] * fields[0]
        for g in range(1, 8):
            acc = acc + blocks[r, 8 * g : 8 * g + 8, :] * fields[g]
        parts.append(acc)
    return fold_sublanes(parts)


def coarse_off_apply(off, fields):
    parts = []
    for ab in range(8):
        rows = slice(8 * ab, 8 * ab + 8)
        acc = off[rows, 0:8, :] * fields[0][None]
        for g in range(1, 8):
            acc = acc + off[rows, 8 * g : 8 * g + 8, :] * fields[g][None]
        parts.append(fold_sublanes([acc[i] for i in range(8)]))
    return fold_lanes(parts)


def restrict_kernel(flags, columns, diag, off, rhs, x, up, down, cross, agg, cinv, coarse_rhs, out, fields, res, acc):
    gather_fine(flags, columns, x, up, down, cross, fields)
    residual_into(res, rhs, diag, off, fields, acc)
    r = res[...]
    hi = r.astype(jnp.bfloat16)
    rest = r - hi.astype(F32)
    mid = rest.astype(jnp.bfloat16)
    low = (rest - mid.astype(F32)).astype(jnp.bfloat16)
    parts = jnp.concatenate([hi, mid, low], axis=0)
    row_of = jnp.broadcast_to(agg[...], (LANES, LANES))
    select = jnp.where(row_of == (iota((LANES, LANES), 0) & 15), 1.0, 0.0).astype(jnp.bfloat16)
    sums = lax.dot_general(parts, select, (((1,), (1,)), ((), ())), preferred_element_type=F32)
    full = sums[0:64] + (sums[64:128] + sums[128:192])
    coarse_rhs[...] = pack_rows(full)
    out[...] = damping * small_apply(cinv, [full[8 * g : 8 * g + 8] for g in range(8)])


def coarse_step(flags, columns, cdiag, coff, cinv, coarse_rhs, u, up, down, cross):
    left, right = neighbours(flags, up[...], down[...], cross[...])
    places = jnp.broadcast_to(columns[...], (8, LANES))
    inner = places & 15
    mine = u[...]
    fields = []
    for g in range(8):
        lane = inner + 16 * g
        fields.append(
            jnp.where(
                places < 0,
                take_lanes(left, lane),
                jnp.where(places < 16, take_lanes(mine, lane), take_lanes(right, lane)),
            )
        )
    total = small_apply(cdiag, spread_rows(mine)) + coarse_off_apply(coff, fields)
    return mine + damping * small_apply(cinv, spread_rows(coarse_rhs[...] - total))


def coarse_kernel(flags, columns, cdiag, coff, cinv, coarse_rhs, u, up, down, cross, out):
    out[...] = coarse_step(flags, columns, cdiag, coff, cinv, coarse_rhs, u, up, down, cross)


def prolong_kernel(flags, columns, cdiag, coff, cinv, coarse_rhs, u, up, down, cross, agg, x, out):
    last = coarse_step(flags, columns, cdiag, coff, cinv, coarse_rhs, u, up, down, cross)
    lane = jnp.broadcast_to(agg[...], (8, LANES))
    for g in range(8):
        part = slice(8 * g, 8 * g + 8)
        out[part, :] = x[part, :] + take_lanes(last, lane + 16 * g)


def in_vmem(array):
    return pltpu.with_memory_space_constraint(array, pltpu.VMEM)


VM = pl.BlockSpec(memory_space=pltpu.VMEM)
SM = pl.BlockSpec(memory_space=pltpu.SMEM)


FAR = pl.BlockSpec(memory_space=pltpu.HBM)


def call(kernel, outs, args, scratch=(), smem=False, far=False, limit=4, flops=0, moved=0):
    shapes = [pltpu.VMEM(shape, F32) for shape in outs]
    specs = [FAR if far else VM] * len(args)
    if smem:
        specs[0] = SM
    if far:
        args = [pltpu.with_memory_space_constraint(a, pltpu.HBM) for a in args]
    else:
        args = [a if (smem and i == 0) else in_vmem(a) for i, a in enumerate(args)]
    return pl.pallas_call(
        kernel,
        out_shape=shapes if len(shapes) > 1 else shapes[0],
        in_specs=specs,
        out_specs=[VM] * len(shapes) if len(shapes) > 1 else VM,
        scratch_shapes=list(scratch),
        compiler_params=pltpu.CompilerParams(vmem_limit_bytes=limit * 1024 * 1024),
        cost_estimate=pl.CostEstimate(flops=flops, bytes_accessed=moved, transcendentals=0) if flops else None,
    )(*args)


def shards(
    right_side,
    fine_diag,
    fine_off,
    fine_inv,
    fine_columns,
    aggregate,
    coarse_diag,
    coarse_off,
    coarse_inv,
    coarse_columns,
):
    size, rows = right_side.shape
    slots = fine_off.shape[0]
    own_rows = coarse_diag.shape[2]
    cslots = coarse_off.shape[0]
    count = lax.axis_size(AXES)
    device = lax.axis_index(AXES)
    ways = routes(count)
    flags = jnp.stack(
        [
            device % LINE == 0,
            device % LINE == LINE - 1,
            device == 0,
            device == count - 1,
        ]
    ).astype(jnp.int32)
    columns = fine_columns - device * rows
    ccolumns = (coarse_columns - device * own_rows).reshape(1, cslots * own_rows)
    agg = aggregate.reshape(1, rows)
    full = (size, rows)
    packed = (8, LANES)
    bf16 = jnp.bfloat16
    scratch = [
        pltpu.VMEM((slots + 1,) + full, F32),
        pltpu.VMEM(full, F32),
        pltpu.VMEM((size, 8, LANES), F32),
    ]

    def sweep(x):
        return call(
            sweep_kernel,
            [full],
            [flags, columns, fine_diag, fine_off, fine_inv, right_side, x, *exchange(x, ways)],
            scratch,
            smem=True,
        )

    x, fine_inv, right_side = call(
        first_kernel,
        [full, fine_inv.shape, full],
        [fine_inv, right_side],
        [pltpu.VMEM(fine_inv.shape, bf16), pltpu.SemaphoreType.DMA(()), pltpu.SemaphoreType.DMA((8,))],
        far=True,
    )
    fine_diag, fine_off = call(
        widen_kernel,
        [fine_diag.shape, fine_off.shape],
        [fine_diag, fine_off],
        [pltpu.VMEM((slots + 1, size, size, rows), bf16), pltpu.SemaphoreType.DMA((slots + 1,))],
        far=True,
        limit=12,
    )
    coarse = [
        jnp.transpose(coarse_diag, (0, 2, 1)),
        jnp.transpose(coarse_off, (0, 1, 3, 2)),
        jnp.transpose(coarse_inv, (0, 2, 1)),
    ]
    turned = (8, size, LANES)
    cdiag, coff, cinv = call(
        coarse_prep_kernel,
        [turned, (size, size, LANES), turned],
        coarse,
        [pltpu.VMEM(c.shape, bf16) for c in coarse] + [pltpu.SemaphoreType.DMA((3,))],
        far=True,
        limit=8,
    )
    for cycle in range(CYCLES):
        for step in range(SWEEPS):
            if cycle or step:
                x = sweep(x)
        crhs, u = call(
            restrict_kernel,
            [packed, packed],
            [flags, columns, fine_diag, fine_off, right_side, x, *exchange(x, ways), agg, cinv],
            scratch,
            smem=True,
        )
        for step in range(1, CSWEEPS):
            base = [flags, ccolumns, cdiag, coff, cinv, crhs, u, *exchange(u, ways)]
            if step < CSWEEPS - 1:
                u = call(coarse_kernel, [packed], base, smem=True)
            else:
                x = call(prolong_kernel, [full], base + [agg, x], smem=True)
        for step in range(SWEEPS):
            x = sweep(x)
    return x


def solution(mesh):
    placed = (
        P(None, AXES),
        P(None, None, AXES),
        P(None, None, None, AXES),
        P(None, None, AXES),
        P(None, AXES),
        P(AXES),
        P(None, None, AXES),
        P(None, None, None, AXES),
        P(None, None, AXES),
        P(None, AXES),
    )
    return jax.shard_map(
        shards, mesh=mesh, in_specs=placed, out_specs=P(None, AXES), check_vma=False
    )
```

```python
import jax
import jax.numpy as jnp
from jax import lax
from jax.experimental import pallas as pl
from jax.experimental.pallas import tpu as pltpu
from jax.sharding import PartitionSpec as P

SWEEPS = 2
CSWEEPS = 4
CYCLES = 2
AXES = ("brick", "group")
LINE = 4

damping = 0.7
LANES = 128
F32 = jnp.float32


def routes(count):
    lines = count // LINE
    cross, down, up = [], [], []
    for i in range(count):
        base = i - i % LINE
        up.append((i, base + (i + 1) % LINE))
        down.append((i, base + (i - 1) % LINE))
    for k in range(lines - 1):
        a, b = LINE * k + LINE - 1, LINE * k + LINE
        cross += [(a, b), (b, a)]
    for k in range(1, lines - 1):
        a, b = LINE * k + 1, LINE * k + 2
        cross += [(a, b), (b, a)]
    last = count - 1
    cross += [(0, 1), (1, 2), (2, 0), (last - 2, last - 1), (last - 1, last), (last, last - 2)]
    return cross, down, up


def exchange(field, ways):
    cross, down, up = ways
    cross = lax.ppermute(field, AXES, cross)
    down = lax.ppermute(field, AXES, down)
    up = lax.ppermute(field, AXES, up)
    return cross, down, up


def iota(shape, dim):
    return lax.broadcasted_iota(jnp.int32, shape, dim)


def fold_sublanes(parts):
    rows = iota(parts[0].shape, 0)
    shift = 4
    while shift:
        low = (rows & shift) == 0
        parts = [
            jnp.where(low, a, b) + pltpu.roll(jnp.where(low, b, a), 4 if shift == 4 else (8 - shift), 0)
            if shift == 4
            else fold_pair(a, b, low, shift, 0)
            for a, b in zip(parts[:shift], parts[shift:])
        ]
        shift //= 2
    return parts[0]


def fold_pair(a, b, low, shift, axis):
    size = a.shape[axis]
    own = jnp.where(low, a, b)
    other = jnp.where(low, b, a)
    return own + jnp.where(
        low, pltpu.roll(other, size - shift, axis), pltpu.roll(other, shift, axis)
    )


def fold_lanes(parts):
    lanes = iota(parts[0].shape, 1)
    shift, half = 64, 4
    while half:
        low = (lanes & shift) == 0
        if shift == 64:
            parts = [
                jnp.where(low, a, b) + pltpu.roll(jnp.where(low, b, a), 64, 1)
                for a, b in zip(parts[:half], parts[half:])
            ]
        else:
            parts = [fold_pair(a, b, low, shift, 1) for a, b in zip(parts[:half], parts[half:])]
        shift //= 2
        half //= 2
    return parts[0]


def take_lanes(field, places):
    return jnp.take_along_axis(field, places, axis=1, mode="promise_in_bounds")


def place_on_line():
    return lax.axis_index(AXES), lax.axis_size(AXES)


def neighbours(cross, down, up):
    device, count = place_on_line()
    spot = lax.rem(device, LINE)
    left = jnp.where(spot == 0, cross, up)
    right = jnp.where(spot == LINE - 1, cross, down)
    left = jnp.where(device == 0, 0.0, left)
    right = jnp.where(device == count - 1, 0.0, right)
    return left, right


def outer_lanes(shape):
    lanes = iota(shape, len(shape) - 1)
    return (lanes < 32) | (lanes >= 96)


def split_field(top, bottom):
    outer = outer_lanes(top.shape)
    turned = pltpu.roll(bottom, 64, top.ndim - 1)
    return jnp.where(outer, top, turned), jnp.where(outer, turned, top)


def join_field(rim, core):
    outer = outer_lanes(rim.shape)
    return jnp.where(outer, rim, core), pltpu.roll(jnp.where(outer, core, rim), 64, 1)


def pack_halves(top, bottom, outer):
    return jnp.where(outer, top, bottom) + pltpu.roll(jnp.where(outer, bottom, top), 64, 1)


def fold_all(acc, outer):
    rows = [fold_sublanes([acc[8 * k + i] for i in range(8)]) for k in range(8)]
    return [pack_halves(rows[k], rows[k + 4], outer) for k in range(4)]


def apply_slots(blocks, fields, acc):
    step = 16

    def body(ab, carry):
        rows = pl.ds(pl.multiple_of(ab * step, step), step)
        total = jnp.zeros((step, 8, LANES), F32)
        for slot in range(fields.shape[0]):
            for g in range(4):
                part = slice(8 * g, 8 * g + 8)
                total = total + blocks[slot, rows, part, :] * fields[slot, part, :][None]
        acc[rows] = total
        return carry

    lax.fori_loop(0, 64 // step, body, 0)


def apply_one(blocks, parts, outer):
    out = []
    for k in range(8):
        rows = slice(8 * k, 8 * k + 8)
        total = blocks[rows, 0:8, :] * parts[0][None]
        for g in range(1, 4):
            total = total + blocks[rows, 8 * g : 8 * g + 8, :] * parts[g][None]
        out.append(fold_sublanes([total[i] for i in range(8)]))
    return [pack_halves(out[k], out[k + 4], outer) for k in range(4)]


def home_lanes(is_rim):
    outer = outer_lanes((8, LANES))
    return outer if is_rim else jnp.logical_not(outer)


def gather_fields(columns, own, rim, core, outside, fields):
    is_rim = outside is not None
    home = home_lanes(is_rim)
    slots = fields.shape[0] - 1
    places = [jnp.broadcast_to(columns[s : s + 1, :], (8, LANES)) for s in range(slots)]
    lane = [jnp.where(home, p, p + 64) & (LANES - 1) for p in places]
    inner = [((p + 32) & 64) != 0 for p in places]
    inside = [(p >= 0) & (p < LANES) for p in places]
    for g in range(4):
        part = slice(8 * g, 8 * g + 8)
        fields[0, part, :] = own[part, :]
        if outside is not None:
            left, right = neighbours(*[o[part, :] for o in outside])
            beyond = jnp.where((iota((8, LANES), 1) & 32) == 0, right, left)
        for s in range(slots):
            edge = take_lanes(rim[part, :], lane[s])
            if outside is not None:
                edge = jnp.where(inside[s], edge, take_lanes(beyond, lane[s]))
            middle = take_lanes(core[part, :], lane[s])
            fields[s + 1, part, :] = jnp.where(inner[s], middle, edge)


def part_residual(columns, blocks, rhs, own, rim, core, outside, fields, acc):
    gather_fields(columns, own, rim, core, outside, fields)
    apply_slots(blocks, fields, acc)
    total = fold_all(acc, home_lanes(outside is not None))
    return [rhs[8 * g : 8 * g + 8, :] - total[g] for g in range(4)]


def part_sweep(columns, blocks, inv, rhs, own, rim, core, outside, fields, acc):
    res = part_residual(columns, blocks, rhs, own, rim, core, outside, fields, acc)
    step = apply_one(inv, res, home_lanes(outside is not None))
    return [own[8 * g : 8 * g + 8, :] + damping * step[g] for g in range(4)]


def rim_kernel(columns, blocks, inv, rhs, rim, core, cross, down, up, out, fields, acc):
    new = part_sweep(columns, blocks, inv, rhs, rim, rim, core, (cross, down, up), fields, acc)
    for g in range(4):
        out[8 * g : 8 * g + 8, :] = new[g]


def core_kernel(columns, blocks, inv, rhs, rim, core, out, fields, acc):
    new = part_sweep(columns, blocks, inv, rhs, core, rim, core, None, fields, acc)
    for g in range(4):
        out[8 * g : 8 * g + 8, :] = new[g]


def core_residual_kernel(columns, blocks, rhs, rim, core, out, fields, acc):
    res = part_residual(columns, blocks, rhs, core, rim, core, None, fields, acc)
    for g in range(4):
        out[8 * g : 8 * g + 8, :] = res[g]


def last_kernel(columns, blocks, inv, rhs, rim, core, cross, down, up, new_core, out, fields, acc, held, sem):
    new = part_sweep(columns, blocks, inv, rhs, rim, rim, core, (cross, down, up), fields, acc)
    for g in range(4):
        part = slice(8 * g, 8 * g + 8)
        top, bottom = join_field(new[g], new_core[part, :])
        held[part, :] = top
        held[32 + 8 * g : 40 + 8 * g, :] = bottom
    copy = pltpu.make_async_copy(held, out, sem)
    copy.start()
    copy.wait()


def first_kernel(
    inv, rhs, columns, agg, ccolumns,
    rim, core, rim_inv, core_inv, rim_rhs, core_rhs, rim_columns, core_columns, near,
    held, rhs_in, col_in, agg_in, ccol_in, sems,
):
    device, _ = place_on_line()
    copies = [pltpu.make_async_copy(rhs, rhs_in, sems.at[8])] + [
        pltpu.make_async_copy(inv.at[pl.ds(8 * k, 8)], held.at[pl.ds(8 * k, 8)], sems.at[k])
        for k in range(8)
    ]
    small = [
        pltpu.make_async_copy(columns, col_in, sems.at[9]),
        pltpu.make_async_copy(agg, agg_in, sems.at[10]),
        pltpu.make_async_copy(ccolumns, ccol_in, sems.at[11]),
    ]
    for copy in copies + small:
        copy.start()
    copies[0].wait()
    own = ([], [])
    for g in range(4):
        part = slice(8 * g, 8 * g + 8)
        edge, middle = split_field(rhs_in[part, :], rhs_in[32 + 8 * g : 40 + 8 * g, :])
        rim_rhs[part, :] = edge
        core_rhs[part, :] = middle
        own[0].append(edge)
        own[1].append(middle)
    sums = ([], [])
    for k in range(8):
        copies[k + 1].wait()
        rows = slice(8 * k, 8 * k + 8)
        wide = held[rows].astype(F32)
        both = split_field(wide[:, :32], wide[:, 32:])
        for blocks, piece, parts, kept in zip((rim_inv, core_inv), both, own, sums):
            blocks[rows] = piece
            total = piece[:, 0:8] * parts[0][None]
            for g in range(1, 4):
                total = total + piece[:, 8 * g : 8 * g + 8] * parts[g][None]
            kept.append(fold_sublanes([total[i] for i in range(8)]))
    for out, kept, home in ((rim, sums[0], True), (core, sums[1], False)):
        for g in range(4):
            total = pack_halves(kept[g], kept[g + 4], home_lanes(home))
            out[8 * g : 8 * g + 8, :] = damping * total
    for copy in small:
        copy.wait()
    slots = columns.shape[0]
    rows = iota((8, LANES), 0)
    table = jnp.broadcast_to(agg_in[...], (8, LANES))
    for s in range(slots):
        table = jnp.where(
            rows == s, jnp.broadcast_to(col_in[s : s + 1, :] - device * LANES, (8, LANES)), table
        )
    turned = pltpu.roll(table, 64, 1)
    outer = outer_lanes((8, LANES))
    rim_columns[...] = jnp.where(outer, table, turned)
    core_columns[...] = jnp.where(outer, turned, table)
    count = ccol_in.shape[1]
    tiled = jnp.concatenate([ccol_in[...]] * (LANES // count), axis=1)
    chosen = jnp.where(rows == iota((8, LANES), 1) // count, tiled - device * count, 0)
    near[...] = jnp.broadcast_to(jnp.sum(chosen, axis=0, keepdims=True), (8, LANES))


def widen_kernel(diag, off, rim_out, core_out, held, sems):
    slots = off.shape[0] + 1
    copies = [pltpu.make_async_copy(diag, held.at[0], sems.at[0])]
    for s in range(1, slots):
        copies.append(pltpu.make_async_copy(off.at[s - 1], held.at[s], sems.at[s]))
    for copy in copies:
        copy.start()
    for s in range(slots):
        copies[s].wait()

        def body(ab, carry):
            rows = pl.ds(pl.multiple_of(ab * 8, 8), 8)
            wide = held[s, rows].astype(F32)
            rim_out[s, rows], core_out[s, rows] = split_field(wide[:, :32], wide[:, 32:])
            return carry

        lax.fori_loop(0, 8, body, 0)


def turn(block):
    return jnp.transpose(block.astype(F32), (1, 0))


def coarse_ends_kernel(diag, inv, diag_out, inv_out):
    for src, dst in ((inv, inv_out), (diag, diag_out)):
        for r in range(8):
            dst[r] = turn(jnp.concatenate([src[8 * h + r] for h in range(8)], axis=0))


def coarse_off_kernel(off, off_out):
    slots, size = off.shape[:2]

    def body(i, carry):
        for j in range(8):
            a = 8 * i + j
            off_out[a] = turn(jnp.concatenate([off[s, a] for s in range(slots)], axis=0))
        return carry

    lax.fori_loop(0, size // 8, body, 0)


def pack_rows(full):
    group = iota((8, LANES), 1) // 16
    out = full[0:8, :]
    for g in range(1, 8):
        out = jnp.where(group == g, full[8 * g : 8 * g + 8, :], out)
    return out


def spread_rows(packed):
    lane = iota((8, LANES), 1) & 15
    return [take_lanes(packed, lane + 16 * h) for h in range(8)]


def small_apply(blocks, fields):
    parts = []
    for r in range(8):
        acc = blocks[r, 0:8, :] * fields[0]
        for g in range(1, 8):
            acc = acc + blocks[r, 8 * g : 8 * g + 8, :] * fields[g]
        parts.append(acc)
    return fold_sublanes(parts)


def coarse_off_apply(off, fields):
    parts = []
    for ab in range(8):
        rows = slice(8 * ab, 8 * ab + 8)
        acc = off[rows, 0:8, :] * fields[0][None]
        for g in range(1, 8):
            acc = acc + off[rows, 8 * g : 8 * g + 8, :] * fields[g][None]
        parts.append(fold_sublanes([acc[i] for i in range(8)]))
    return fold_lanes(parts)


def restrict_kernel(
    columns, blocks, rhs, rim, core, core_res, cross, down, up, core_columns, cinv,
    coarse_rhs, out, fields, acc,
):
    res = part_residual(columns, blocks, rhs, rim, rim, core, (cross, down, up), fields, acc)
    inner = core_res[...]
    edge = jnp.concatenate(res, axis=0)
    r = jnp.concatenate(join_field(edge, inner), axis=0)
    hi = r.astype(jnp.bfloat16)
    rest = r - hi.astype(F32)
    mid = rest.astype(jnp.bfloat16)
    last = (rest - mid.astype(F32)).astype(jnp.bfloat16)
    parts = jnp.concatenate([hi, mid, last], axis=0)
    slots = fields.shape[0] - 1
    agg = jnp.where(
        outer_lanes((1, LANES)), columns[slots : slots + 1, :], core_columns[slots : slots + 1, :]
    )
    row_of = jnp.broadcast_to(agg, (LANES, LANES))
    select = jnp.where(row_of == (iota((LANES, LANES), 0) & 15), 1.0, 0.0).astype(jnp.bfloat16)
    sums = lax.dot_general(parts, select, (((1,), (1,)), ((), ())), preferred_element_type=F32)
    full = sums[0:64] + (sums[64:128] + sums[128:192])
    coarse_rhs[...] = pack_rows(full)
    out[...] = damping * small_apply(cinv, [full[8 * g : 8 * g + 8] for g in range(8)])


def coarse_step(places, cdiag, coff, cinv, coarse_rhs, u, cross, down, up):
    left, right = neighbours(cross[...], down[...], up[...])
    places = places[...]
    inner = places & 15
    mine = u[...]
    fields = []
    for g in range(8):
        lane = inner + 16 * g
        fields.append(
            jnp.where(
                places < 0,
                take_lanes(left, lane),
                jnp.where(places < 16, take_lanes(mine, lane), take_lanes(right, lane)),
            )
        )
    total = small_apply(cdiag, spread_rows(mine)) + coarse_off_apply(coff, fields)
    return mine + damping * small_apply(cinv, spread_rows(coarse_rhs[...] - total))


def coarse_kernel(places, cdiag, coff, cinv, coarse_rhs, u, cross, down, up, out):
    out[...] = coarse_step(places, cdiag, coff, cinv, coarse_rhs, u, cross, down, up)


def prolong_kernel(
    places, cdiag, coff, cinv, coarse_rhs, u, cross, down, up, rim_columns, core_columns, rim, core,
    rim_out, core_out,
):
    last = coarse_step(places, cdiag, coff, cinv, coarse_rhs, u, cross, down, up)
    row = 6
    tables = ((rim_columns, rim, rim_out, True), (core_columns, core, core_out, False))
    for table, old, out, is_rim in tables:
        lane = jnp.broadcast_to(table[row : row + 1, :], (8, LANES))
        lane = jnp.where(home_lanes(is_rim), lane, lane + 64)
        for g in range(4):
            part = slice(8 * g, 8 * g + 8)
            out[part, :] = old[part, :] + take_lanes(last, lane + 16 * g)


def in_vmem(array):
    return pltpu.with_memory_space_constraint(array, pltpu.VMEM)


VM = pl.BlockSpec(memory_space=pltpu.VMEM)
FAR = pl.BlockSpec(memory_space=pltpu.HBM)


def call(kernel, outs, args, scratch=(), far=False, limit=4, flops=0, moved=0):
    shapes = [pltpu.VMEM(o[0], o[1]) if isinstance(o[0], tuple) else pltpu.VMEM(o, F32) for o in outs]
    place = pltpu.HBM if far else pltpu.VMEM
    return pl.pallas_call(
        kernel,
        out_shape=shapes if len(shapes) > 1 else shapes[0],
        in_specs=[pl.BlockSpec(memory_space=place)] * len(args),
        out_specs=[VM] * len(shapes) if len(shapes) > 1 else VM,
        scratch_shapes=list(scratch),
        compiler_params=pltpu.CompilerParams(vmem_limit_bytes=limit * 1024 * 1024),
    )(*[pltpu.with_memory_space_constraint(a, place) for a in args])


def shards(
    right_side,
    fine_diag,
    fine_off,
    fine_inv,
    fine_columns,
    aggregate,
    coarse_diag,
    coarse_off,
    coarse_inv,
    coarse_columns,
):
    size, rows = right_side.shape
    slots = fine_off.shape[0]
    own_rows = coarse_diag.shape[2]
    ways = routes(lax.axis_size(AXES))
    bf16 = jnp.bfloat16
    i32 = jnp.int32
    full = (size, rows)
    half = (size // 2, rows)
    packed = (8, LANES)
    table = ((8, LANES), i32)
    blocks = (slots + 1, size, size // 2, rows)
    turned = (8, size, LANES)
    sem = pltpu.SemaphoreType.DMA
    work = [pltpu.VMEM((slots + 1,) + half, F32), pltpu.VMEM((size, 8, LANES), F32)]

    rim, core, rim_inv, core_inv, rim_rhs, core_rhs, rim_cols, core_cols, near = call(
        first_kernel,
        [half, half, blocks[1:], blocks[1:], half, half, table, table, table],
        [fine_inv, right_side, fine_columns, aggregate.reshape(1, rows), coarse_columns],
        [
            pltpu.VMEM(fine_inv.shape, bf16),
            pltpu.VMEM(full, F32),
            pltpu.VMEM((slots, rows), i32),
            pltpu.VMEM((1, rows), i32),
            pltpu.VMEM(coarse_columns.shape, i32),
            sem((12,)),
        ],
        far=True,
    )
    sent = exchange(rim, ways)
    rim_blocks, core_blocks = call(
        widen_kernel,
        [blocks, blocks],
        [fine_diag, fine_off],
        [pltpu.VMEM((slots + 1, size, size, rows), bf16), sem((slots + 1,))],
        far=True,
        limit=12,
    )
    ends = [jnp.transpose(coarse_diag, (0, 2, 1)), jnp.transpose(coarse_inv, (0, 2, 1))]
    cdiag, cinv = call(coarse_ends_kernel, [turned, turned], ends)
    others = jnp.transpose(coarse_off, (0, 1, 3, 2))
    coff = call(coarse_off_kernel, [(size, size, LANES)], [others])

    def sweep_core(rim, core):
        return call(core_kernel, [half], [core_cols, core_blocks, core_inv, core_rhs, rim, core], work)

    def sweep_rim(rim, core, sent):
        args = [rim_cols, rim_blocks, rim_inv, rim_rhs, rim, core, *sent]
        return call(rim_kernel, [half], args, work)

    for cycle in range(CYCLES):
        for step in range(SWEEPS):
            if cycle or step:
                rim, core = sweep_rim(rim, core, sent), sweep_core(rim, core)
                sent = exchange(rim, ways)
        core_res = call(
            core_residual_kernel, [half], [core_cols, core_blocks, core_rhs, rim, core], work
        )
        crhs, u = call(
            restrict_kernel,
            [packed, packed],
            [rim_cols, rim_blocks, rim_rhs, rim, core, core_res, *sent, core_cols, cinv],
            work,
        )
        for step in range(1, CSWEEPS):
            base = [near, cdiag, coff, cinv, crhs, u, *exchange(u, ways)]
            if step < CSWEEPS - 1:
                u = call(coarse_kernel, [packed], base)
            else:
                rim, core = call(prolong_kernel, [half, half], base + [rim_cols, core_cols, rim, core])
        sent = exchange(rim, ways)
        for step in range(SWEEPS):
            if cycle == CYCLES - 1 and step == SWEEPS - 1:
                break
            rim, core = sweep_rim(rim, core, sent), sweep_core(rim, core)
            sent = exchange(rim, ways)
    args = [rim_cols, rim_blocks, rim_inv, rim_rhs, rim, core, *sent, sweep_core(rim, core)]
    return pl.pallas_call(
        last_kernel,
        out_shape=pltpu.HBM(full, F32),
        in_specs=[VM] * len(args),
        out_specs=FAR,
        scratch_shapes=work + [pltpu.VMEM(full, F32), sem(())],
        compiler_params=pltpu.CompilerParams(vmem_limit_bytes=4 * 1024 * 1024),
    )(*[in_vmem(a) for a in args])


def solution(mesh):
    placed = (
        P(None, AXES),
        P(None, None, AXES),
        P(None, None, None, AXES),
        P(None, None, AXES),
        P(None, AXES),
        P(AXES),
        P(None, None, AXES),
        P(None, None, None, AXES),
        P(None, None, AXES),
        P(None, AXES),
    )
    return jax.shard_map(
        shards, mesh=mesh, in_specs=placed, out_specs=P(None, AXES), check_vma=False
    )
```

```python
import jax
import jax.numpy as jnp
from jax import lax
from jax.experimental import pallas as pl
from jax.experimental.pallas import tpu as pltpu
from jax.sharding import PartitionSpec as P

SWEEPS = 2
CSWEEPS = 4
CYCLES = 2
AXES = ("brick", "group")
LINE = 4

damping = 0.7
LANES = 128
F32 = jnp.float32


def routes(count):
    last = count - 1
    cross = []
    for i in range(3, last, 2):
        if i + 1 < last - 1:
            cross += [(i, i + 1), (i + 1, i)]
    cross += [(0, 1), (1, 2), (2, 0), (last - 2, last - 1), (last - 1, last), (last, last - 2)]
    pair = [(i, i ^ 1) for i in range(count)]
    mend = []
    for i in range(count):
        spot = i % LINE
        if spot in (0, LINE - 1):
            mend.append((i, i ^ LINE))
        else:
            low = (i // LINE) % LINE in (0, LINE - 1)
            back = spot == 2
            mend.append((i, i - 1 if low and back else i + 1 if not low and not back else i ^ LINE))
    for way in (mend, pair, cross):
        assert sorted(t for _, t in way) == sorted(f for f, _ in way) == list(range(count))
    return mend, pair, cross


def exchange(field, ways):
    return [lax.ppermute(field, AXES, way) for way in ways]


def iota(shape, dim):
    return lax.broadcasted_iota(jnp.int32, shape, dim)


def fold_sublanes(parts):
    rows = iota(parts[0].shape, 0)
    shift = 4
    while shift:
        low = (rows & shift) == 0
        parts = [
            jnp.where(low, a, b) + pltpu.roll(jnp.where(low, b, a), 4 if shift == 4 else (8 - shift), 0)
            if shift == 4
            else fold_pair(a, b, low, shift, 0)
            for a, b in zip(parts[:shift], parts[shift:])
        ]
        shift //= 2
    return parts[0]


def fold_pair(a, b, low, shift, axis):
    size = a.shape[axis]
    own = jnp.where(low, a, b)
    other = jnp.where(low, b, a)
    return own + jnp.where(
        low, pltpu.roll(other, size - shift, axis), pltpu.roll(other, shift, axis)
    )


def take_lanes(field, places):
    return jnp.take_along_axis(field, places, axis=1, mode="promise_in_bounds")


def place_on_line():
    return lax.axis_index(AXES), lax.axis_size(AXES)


def neighbours(mend, pair, cross):
    device, count = place_on_line()
    even = lax.rem(device, 2) == 0
    ends = (device == 1) | (device == count - 3)
    left = jnp.where(even, cross, pair)
    right = jnp.where(even, pair, jnp.where(ends, mend, cross))
    left = jnp.where(device == 0, 0.0, left)
    right = jnp.where(device == count - 1, 0.0, right)
    return left, right


def outer_lanes(shape):
    lanes = iota(shape, len(shape) - 1)
    return (lanes < 32) | (lanes >= 96)


def split_field(top, bottom):
    outer = outer_lanes(top.shape)
    turned = pltpu.roll(bottom, 64, top.ndim - 1)
    return jnp.where(outer, top, turned), jnp.where(outer, turned, top)


def join_field(rim, core):
    outer = outer_lanes(rim.shape)
    return jnp.where(outer, rim, core), pltpu.roll(jnp.where(outer, core, rim), 64, 1)


def pack_halves(top, bottom, outer):
    return jnp.where(outer, top, bottom) + pltpu.roll(jnp.where(outer, bottom, top), 64, 1)


def fold_all(acc, outer):
    rows = [fold_sublanes([acc[8 * k + i] for i in range(8)]) for k in range(8)]
    return [pack_halves(rows[k], rows[k + 4], outer) for k in range(4)]


def apply_slots(blocks, fields, acc, lead=None):
    step = 16 if blocks.dtype == jnp.bfloat16 else 32
    skip = 0 if lead is None else 1

    def body(ab, carry):
        rows = pl.ds(pl.multiple_of(ab * step, step), step)
        total = jnp.zeros((step, 8, LANES), F32) if lead is None else lead[rows]
        for slot in range(fields.shape[0]):
            for g in range(2):
                piece = blocks[slot + skip, rows, 16 * g : 16 * g + 16, :].astype(F32)
                total = total + piece[:, :8] * fields[slot, 16 * g : 16 * g + 8, :][None]
                total = total + piece[:, 8:] * fields[slot, 16 * g + 8 : 16 * g + 16, :][None]
        acc[rows] = total
        return carry

    lax.fori_loop(0, 64 // step, body, 0)


def apply_one(blocks, parts, outer):
    out = []
    for k in range(8):
        rows = slice(8 * k, 8 * k + 8)
        total = jnp.zeros((8, 8, LANES), F32)
        for g in range(2):
            piece = blocks[rows, 16 * g : 16 * g + 16, :].astype(F32)
            total = total + piece[:, :8] * parts[2 * g][None]
            total = total + piece[:, 8:] * parts[2 * g + 1][None]
        out.append(fold_sublanes([total[i] for i in range(8)]))
    return [pack_halves(out[k], out[k + 4], outer) for k in range(4)]


def home_lanes(is_rim):
    outer = outer_lanes((8, LANES))
    return outer if is_rim else jnp.logical_not(outer)


def lanes_of(columns, slots, is_rim):
    home = home_lanes(is_rim)
    places = [jnp.broadcast_to(columns[s : s + 1, :], (8, LANES)) for s in range(slots)]
    return places, [jnp.where(home, p, p + 64) & (LANES - 1) for p in places]


def gather_inside(columns, slots, is_rim, rim, core, fields, first):
    places, lane = lanes_of(columns, slots, is_rim)
    inner = [((p + 32) & 64) != 0 for p in places]
    for g in range(4):
        part = slice(8 * g, 8 * g + 8)
        for s in range(slots):
            edge = take_lanes(rim[part, :], lane[s])
            middle = take_lanes(core[part, :], lane[s])
            fields[first + s, part, :] = jnp.where(inner[s], middle, edge)


def gather_outside(columns, sent, inside, fields):
    slots = fields.shape[0]
    places, lane = lanes_of(columns, slots, True)
    own = [(p >= 0) & (p < LANES) for p in places]
    for g in range(4):
        part = slice(8 * g, 8 * g + 8)
        left, right = neighbours(*[o[part, :] for o in sent])
        beyond = jnp.where((iota((8, LANES), 1) & 32) == 0, right, left)
        for s in range(slots):
            fields[s, part, :] = jnp.where(own[s], inside[s, part, :], take_lanes(beyond, lane[s]))


def rim_residual(columns, blocks, rhs, inside, lead, sent, fields, acc):
    gather_outside(columns, sent, inside, fields)
    apply_slots(blocks, fields, acc, lead)
    total = fold_all(acc, home_lanes(True))
    return [rhs[8 * g : 8 * g + 8, :] - total[g] for g in range(4)]


def rim_sweep(columns, blocks, inv, rhs, rim, inside, lead, sent, fields, acc):
    res = rim_residual(columns, blocks, rhs, inside, lead, sent, fields, acc)
    step = apply_one(inv, res, home_lanes(True))
    return [rim[8 * g : 8 * g + 8, :] + damping * step[g] for g in range(4)]


def rim_kernel(columns, blocks, inv, rhs, rim, inside, lead, mend, pair, cross, out, fields, acc):
    sent = (mend, pair, cross)
    new = rim_sweep(columns, blocks, inv, rhs, rim, inside, lead, sent, fields, acc)
    for g in range(4):
        out[8 * g : 8 * g + 8, :] = new[g]


def core_residual(columns, blocks, rhs, rim, core, rim_columns, rim_blocks, inside, lead, fields, acc):
    slots = inside.shape[0]
    gather_inside(rim_columns, slots, True, rim, core, inside, 0)
    for k in range(8):
        rows = slice(8 * k, 8 * k + 8)
        total = rim_blocks[0, rows, 0:8, :] * rim[0:8, :][None]
        for g in range(1, 4):
            part = slice(8 * g, 8 * g + 8)
            total = total + rim_blocks[0, rows, part, :] * rim[part, :][None]
        lead[rows] = total
    fields[0] = core[...]
    gather_inside(columns, slots, False, rim, core, fields, 1)
    apply_slots(blocks, fields, acc)
    total = fold_all(acc, home_lanes(False))
    return [rhs[8 * g : 8 * g + 8, :] - total[g] for g in range(4)]


def core_kernel(
    columns, blocks, rhs, rim, core, rim_columns, rim_blocks, inv, out, inside, lead, fields, acc
):
    res = core_residual(
        columns, blocks, rhs, rim, core, rim_columns, rim_blocks, inside, lead, fields, acc
    )
    step = apply_one(inv, res, home_lanes(False))
    for g in range(4):
        part = slice(8 * g, 8 * g + 8)
        out[part, :] = core[part, :] + damping * step[g]


def core_residual_kernel(
    columns, blocks, rhs, rim, core, rim_columns, rim_blocks, out, inside, lead, fields, acc
):
    res = core_residual(
        columns, blocks, rhs, rim, core, rim_columns, rim_blocks, inside, lead, fields, acc
    )
    for g in range(4):
        out[8 * g : 8 * g + 8, :] = res[g]


def last_kernel(
    columns, blocks, inv, rhs, rim, inside, lead, mend, pair, cross, new_core,
    out, fields, acc, held, sem,
):
    sent = (mend, pair, cross)
    new = rim_sweep(columns, blocks, inv, rhs, rim, inside, lead, sent, fields, acc)
    for g in range(4):
        part = slice(8 * g, 8 * g + 8)
        top, bottom = join_field(new[g], new_core[part, :])
        held[part, :] = top
        held[32 + 8 * g : 40 + 8 * g, :] = bottom
    copy = pltpu.make_async_copy(held, out, sem)
    copy.start()
    copy.wait()


def first_kernel(
    inv, rhs, columns, agg, ccolumns,
    rim, core, rim_inv, core_inv, rim_rhs, core_rhs, rim_columns, core_columns, near,
    held, rhs_in, col_in, agg_in, ccol_in, sems,
):
    device, _ = place_on_line()
    copies = [pltpu.make_async_copy(rhs, rhs_in, sems.at[8])] + [
        pltpu.make_async_copy(inv.at[pl.ds(8 * k, 8)], held.at[pl.ds(8 * k, 8)], sems.at[k])
        for k in range(8)
    ]
    small = [
        pltpu.make_async_copy(columns, col_in, sems.at[9]),
        pltpu.make_async_copy(agg, agg_in, sems.at[10]),
        pltpu.make_async_copy(ccolumns, ccol_in, sems.at[11]),
    ]
    for copy in copies + small:
        copy.start()
    copies[0].wait()
    own = ([], [])
    for g in range(4):
        part = slice(8 * g, 8 * g + 8)
        edge, middle = split_field(rhs_in[part, :], rhs_in[32 + 8 * g : 40 + 8 * g, :])
        rim_rhs[part, :] = edge
        core_rhs[part, :] = middle
        own[0].append(edge)
        own[1].append(middle)
    sums = ([], [])
    for k in range(8):
        copies[k + 1].wait()
        rows = slice(8 * k, 8 * k + 8)
        both = split_field(held[rows, :32, :], held[rows, 32:, :])
        core_inv[rows] = both[1]
        both = [piece.astype(F32) for piece in both]
        rim_inv[rows] = both[0]
        for piece, parts, kept in zip(both, own, sums):
            total = piece[:, 0:8] * parts[0][None]
            for g in range(1, 4):
                total = total + piece[:, 8 * g : 8 * g + 8] * parts[g][None]
            kept.append(fold_sublanes([total[i] for i in range(8)]))
    for out, kept, home in ((rim, sums[0], True), (core, sums[1], False)):
        for g in range(4):
            total = pack_halves(kept[g], kept[g + 4], home_lanes(home))
            out[8 * g : 8 * g + 8, :] = damping * total
    for copy in small:
        copy.wait()
    slots = columns.shape[0]
    rows = iota((8, LANES), 0)
    table = jnp.broadcast_to(agg_in[...], (8, LANES))
    for s in range(slots):
        table = jnp.where(
            rows == s, jnp.broadcast_to(col_in[s : s + 1, :] - device * LANES, (8, LANES)), table
        )
    turned = pltpu.roll(table, 64, 1)
    outer = outer_lanes((8, LANES))
    rim_columns[...] = jnp.where(outer, table, turned)
    core_columns[...] = jnp.where(outer, turned, table)
    count = ccol_in.shape[1]
    tiled = jnp.concatenate([ccol_in[...]] * (LANES // count), axis=1)
    chosen = jnp.where(rows == iota((8, LANES), 1) // count, tiled - device * count, 0)
    near[...] = jnp.broadcast_to(jnp.sum(chosen, axis=0, keepdims=True), (8, LANES))


def widen_kernel(diag, off, rim_out, core_out, held, sems):
    slots = off.shape[0] + 1
    parts, ahead = 4, 6
    each = diag.shape[0] // parts
    copies = []
    for s in range(slots):
        src = diag if s == 0 else off.at[s - 1]
        for k in range(parts):
            rows = pl.ds(each * k, each)
            copies.append(pltpu.make_async_copy(src.at[rows], held.at[s, rows], sems.at[s, k]))
    for copy in copies[:ahead]:
        copy.start()
    for i, copy in enumerate(copies):
        copy.wait()
        if i + ahead < len(copies):
            copies[i + ahead].start()
        s, k = divmod(i, parts)
        rows = pl.ds(each * k, each)
        rim, core = split_field(held[s, rows, :32, :], held[s, rows, 32:, :])
        rim_out[s, rows] = rim.astype(F32)
        core_out[s, rows] = core


def turn(block):
    return jnp.transpose(block.astype(F32), (1, 0))


def coarse_ends_kernel(diag, inv, diag_out, inv_out):
    for src, dst in ((inv, inv_out), (diag, diag_out)):
        for r in range(8):
            dst[r] = turn(jnp.concatenate([src[8 * h + r] for h in range(8)], axis=0))


def coarse_off_kernel(off, off_out):
    slots, size = off.shape[:2]

    def body(i, carry):
        for j in range(8):
            a = 8 * i + j
            off_out[a] = turn(jnp.concatenate([off[s, a] for s in range(slots)], axis=0))
        return carry

    lax.fori_loop(0, size // 8, body, 0)


def pack_rows(full):
    group = iota((8, LANES), 1) // 16
    out = full[0:8, :]
    for g in range(1, 8):
        out = jnp.where(group == g, full[8 * g : 8 * g + 8, :], out)
    return out


def spread_rows(packed):
    lane = iota((8, LANES), 1) & 15
    return [take_lanes(packed, lane + 16 * h) for h in range(8)]


def small_apply(blocks, fields):
    parts = []
    for r in range(8):
        acc = blocks[r, 0:8, :] * fields[0]
        for g in range(1, 8):
            acc = acc + blocks[r, 8 * g : 8 * g + 8, :] * fields[g]
        parts.append(acc)
    return fold_sublanes(parts)


def coarse_off_apply(off, fields):
    parts = []
    for ab in range(8):
        rows = slice(8 * ab, 8 * ab + 8)
        acc = off[rows, 0:8, :] * fields[0][None]
        for g in range(1, 8):
            acc = acc + off[rows, 8 * g : 8 * g + 8, :] * fields[g][None]
        total = fold_sublanes([acc[i] for i in range(8)])
        for shift in (64, 32, 16):
            total = total + pltpu.roll(total, shift, 1)
        parts.append(total)
    return parts


def restrict_kernel(
    columns, blocks, rhs, core_res, inside, lead, mend, pair, cross, core_columns, cinv,
    coarse_rhs, out, fields, acc,
):
    res = rim_residual(columns, blocks, rhs, inside, lead, (mend, pair, cross), fields, acc)
    inner = core_res[...]
    edge = jnp.concatenate(res, axis=0)
    r = jnp.concatenate(join_field(edge, inner), axis=0)
    hi = r.astype(jnp.bfloat16)
    rest = r - hi.astype(F32)
    mid = rest.astype(jnp.bfloat16)
    last = (rest - mid.astype(F32)).astype(jnp.bfloat16)
    parts = jnp.concatenate([hi, mid, last], axis=0)
    slots = fields.shape[0]
    agg = jnp.where(
        outer_lanes((1, LANES)), columns[slots : slots + 1, :], core_columns[slots : slots + 1, :]
    )
    row_of = jnp.broadcast_to(agg, (LANES, LANES))
    select = jnp.where(row_of == (iota((LANES, LANES), 0) & 15), 1.0, 0.0).astype(jnp.bfloat16)
    sums = lax.dot_general(parts, select, (((1,), (1,)), ((), ())), preferred_element_type=F32)
    full = sums[0:64] + (sums[64:128] + sums[128:192])
    coarse_rhs[...] = pack_rows(full)
    out[...] = damping * small_apply(cinv, [full[8 * g : 8 * g + 8] for g in range(8)])


def coarse_step(places, cdiag, coff, cinv, coarse_rhs, u, mend, pair, cross):
    left, right = neighbours(mend[...], pair[...], cross[...])
    places = places[...]
    inner = places & 15
    mine = u[...]
    fields = []
    for g in range(8):
        lane = inner + 16 * g
        fields.append(
            jnp.where(
                places < 0,
                take_lanes(left, lane),
                jnp.where(places < 16, take_lanes(mine, lane), take_lanes(right, lane)),
            )
        )
    base = spread_rows(coarse_rhs[...] - small_apply(cdiag, spread_rows(mine)))
    total = coarse_off_apply(coff, fields)
    return mine + damping * small_apply(cinv, [a - b for a, b in zip(base, total)])


def coarse_kernel(places, cdiag, coff, cinv, coarse_rhs, u, mend, pair, cross, out):
    out[...] = coarse_step(places, cdiag, coff, cinv, coarse_rhs, u, mend, pair, cross)


def prolong_kernel(
    places, cdiag, coff, cinv, coarse_rhs, u, mend, pair, cross, rim_columns, core_columns, rim, core,
    rim_out, core_out,
):
    last = coarse_step(places, cdiag, coff, cinv, coarse_rhs, u, mend, pair, cross)
    row = 6
    tables = ((rim_columns, rim, rim_out, True), (core_columns, core, core_out, False))
    for table, old, out, is_rim in tables:
        lane = jnp.broadcast_to(table[row : row + 1, :], (8, LANES))
        lane = jnp.where(home_lanes(is_rim), lane, lane + 64)
        for g in range(4):
            part = slice(8 * g, 8 * g + 8)
            out[part, :] = old[part, :] + take_lanes(last, lane + 16 * g)


def in_vmem(array):
    return pltpu.with_memory_space_constraint(array, pltpu.VMEM)


VM = pl.BlockSpec(memory_space=pltpu.VMEM)
FAR = pl.BlockSpec(memory_space=pltpu.HBM)


def call(kernel, outs, args, scratch=(), far=False, limit=4, flops=0, moved=0):
    shapes = [pltpu.VMEM(o[0], o[1]) if isinstance(o[0], tuple) else pltpu.VMEM(o, F32) for o in outs]
    place = pltpu.HBM if far else pltpu.VMEM
    return pl.pallas_call(
        kernel,
        out_shape=shapes if len(shapes) > 1 else shapes[0],
        in_specs=[pl.BlockSpec(memory_space=place)] * len(args),
        out_specs=[VM] * len(shapes) if len(shapes) > 1 else VM,
        scratch_shapes=list(scratch),
        compiler_params=pltpu.CompilerParams(vmem_limit_bytes=limit * 1024 * 1024),
    )(*[pltpu.with_memory_space_constraint(a, place) for a in args])


def shards(
    right_side,
    fine_diag,
    fine_off,
    fine_inv,
    fine_columns,
    aggregate,
    coarse_diag,
    coarse_off,
    coarse_inv,
    coarse_columns,
):
    size, rows = right_side.shape
    slots = fine_off.shape[0]
    own_rows = coarse_diag.shape[2]
    ways = routes(lax.axis_size(AXES))
    bf16 = jnp.bfloat16
    i32 = jnp.int32
    full = (size, rows)
    half = (size // 2, rows)
    packed = (8, LANES)
    table = ((8, LANES), i32)
    blocks = (slots + 1, size, size // 2, rows)
    turned = (8, size, LANES)
    sem = pltpu.SemaphoreType.DMA
    work = [pltpu.VMEM((slots + 1,) + half, F32), pltpu.VMEM((size, 8, LANES), F32)]

    rim, core, rim_inv, core_inv, rim_rhs, core_rhs, rim_cols, core_cols, near = call(
        first_kernel,
        [half, half, blocks[1:], (blocks[1:], bf16), half, half, table, table, table],
        [fine_inv, right_side, fine_columns, aggregate.reshape(1, rows), coarse_columns],
        [
            pltpu.VMEM(fine_inv.shape, bf16),
            pltpu.VMEM(full, F32),
            pltpu.VMEM((slots, rows), i32),
            pltpu.VMEM((1, rows), i32),
            pltpu.VMEM(coarse_columns.shape, i32),
            sem((12,)),
        ],
        far=True,
    )
    rim_blocks, core_blocks = call(
        widen_kernel,
        [blocks, (blocks, bf16)],
        [fine_diag, fine_off],
        [pltpu.VMEM((slots + 1, size, size, rows), bf16), sem((slots + 1, 4))],
        far=True,
        limit=12,
    )
    ends = [jnp.transpose(coarse_diag, (0, 2, 1)), jnp.transpose(coarse_inv, (0, 2, 1))]
    cdiag, cinv = call(coarse_ends_kernel, [turned, turned], ends)
    others = jnp.transpose(coarse_off, (0, 1, 3, 2))
    coff = call(coarse_off_kernel, [(size, size, LANES)], [others])

    rim_work = [pltpu.VMEM((slots,) + half, F32), work[1]]
    ready = [half, (slots,) + half, (size, 8, LANES)]

    def core_args(rim, core):
        return [core_cols, core_blocks, core_rhs, rim, core, rim_cols, rim_blocks]

    def sweep_core(rim, core):
        return call(core_kernel, ready, core_args(rim, core) + [core_inv], work)

    def rim_args(rim, inside, lead, sent):
        return [rim_cols, rim_blocks, rim_inv, rim_rhs, rim, inside, lead, *sent]

    def sweep(rim, core):
        sent = exchange(rim, ways)
        core, inside, lead = sweep_core(rim, core)
        return call(rim_kernel, [half], rim_args(rim, inside, lead, sent), rim_work), core

    for cycle in range(CYCLES):
        for step in range(SWEEPS):
            if cycle or step:
                rim, core = sweep(rim, core)
        sent = exchange(rim, ways)
        core_res, inside, lead = call(core_residual_kernel, ready, core_args(rim, core), work)
        crhs, u = call(
            restrict_kernel,
            [packed, packed],
            [rim_cols, rim_blocks, rim_rhs, core_res, inside, lead, *sent, core_cols, cinv],
            rim_work,
        )
        for step in range(1, CSWEEPS):
            base = [near, cdiag, coff, cinv, crhs, u, *exchange(u, ways)]
            if step < CSWEEPS - 1:
                u = call(coarse_kernel, [packed], base)
            else:
                rim, core = call(prolong_kernel, [half, half], base + [rim_cols, core_cols, rim, core])
        for step in range(SWEEPS - (cycle == CYCLES - 1)):
            rim, core = sweep(rim, core)
    sent = exchange(rim, ways)
    core, inside, lead = sweep_core(rim, core)
    args = rim_args(rim, inside, lead, sent) + [core]
    return pl.pallas_call(
        last_kernel,
        out_shape=pltpu.HBM(full, F32),
        in_specs=[VM] * len(args),
        out_specs=FAR,
        scratch_shapes=rim_work + [pltpu.VMEM(full, F32), sem(())],
        compiler_params=pltpu.CompilerParams(vmem_limit_bytes=4 * 1024 * 1024),
    )(*[in_vmem(a) for a in args])


def solution(mesh):
    placed = (
        P(None, AXES),
        P(None, None, AXES),
        P(None, None, None, AXES),
        P(None, None, AXES),
        P(None, AXES),
        P(AXES),
        P(None, None, AXES),
        P(None, None, None, AXES),
        P(None, None, AXES),
        P(None, AXES),
    )
    return jax.shard_map(
        shards, mesh=mesh, in_specs=placed, out_specs=P(None, AXES), check_vma=False
    )
```

```python
import jax
import jax.numpy as jnp
from jax import lax
from jax.experimental import pallas as pl
from jax.experimental.pallas import tpu as pltpu
from jax.sharding import PartitionSpec as P

SWEEPS = 2
CSWEEPS = 4
CYCLES = 2
AXES = ("brick", "group")
LINE = 4

damping = 0.7
LANES = 128
F32 = jnp.float32


def routes(count):
    last = count - 1
    cross = []
    for i in range(3, last, 2):
        if i + 1 < last - 1:
            cross += [(i, i + 1), (i + 1, i)]
    cross += [(0, 1), (1, 2), (2, 0), (last - 2, last - 1), (last - 1, last), (last, last - 2)]
    pair = [(i, i ^ 1) for i in range(count)]
    mend = []
    for i in range(count):
        spot = i % LINE
        if spot in (0, LINE - 1):
            mend.append((i, i ^ LINE))
        else:
            low = (i // LINE) % LINE in (0, LINE - 1)
            back = spot == 2
            mend.append((i, i - 1 if low and back else i + 1 if not low and not back else i ^ LINE))
    for way in (mend, pair, cross):
        assert sorted(t for _, t in way) == sorted(f for f, _ in way) == list(range(count))
    return mend, pair, cross


def exchange(field, ways):
    return [lax.ppermute(field, AXES, way) for way in ways]


def iota(shape, dim):
    return lax.broadcasted_iota(jnp.int32, shape, dim)


def fold_sublanes(parts):
    rows = iota(parts[0].shape, 0)
    shift = 4
    while shift:
        low = (rows & shift) == 0
        parts = [
            jnp.where(low, a, b) + pltpu.roll(jnp.where(low, b, a), 4 if shift == 4 else (8 - shift), 0)
            if shift == 4
            else fold_pair(a, b, low, shift, 0)
            for a, b in zip(parts[:shift], parts[shift:])
        ]
        shift //= 2
    return parts[0]


def fold_pair(a, b, low, shift, axis):
    size = a.shape[axis]
    own = jnp.where(low, a, b)
    other = jnp.where(low, b, a)
    return own + jnp.where(
        low, pltpu.roll(other, size - shift, axis), pltpu.roll(other, shift, axis)
    )


def take_lanes(field, places):
    return jnp.take_along_axis(field, places, axis=1, mode="promise_in_bounds")


def place_on_line():
    return lax.axis_index(AXES), lax.axis_size(AXES)


def neighbours(mend, pair, cross):
    device, count = place_on_line()
    even = lax.rem(device, 2) == 0
    ends = (device == 1) | (device == count - 3)
    left = jnp.where(even, cross, pair)
    right = jnp.where(even, pair, jnp.where(ends, mend, cross))
    left = jnp.where(device == 0, 0.0, left)
    right = jnp.where(device == count - 1, 0.0, right)
    return left, right


def outer_lanes(shape):
    lanes = iota(shape, len(shape) - 1)
    return (lanes < 32) | (lanes >= 96)


def split_field(top, bottom):
    outer = outer_lanes(top.shape)
    turned = pltpu.roll(bottom, 64, top.ndim - 1)
    return jnp.where(outer, top, turned), jnp.where(outer, turned, top)


def join_field(rim, core):
    outer = outer_lanes(rim.shape)
    return jnp.where(outer, rim, core), pltpu.roll(jnp.where(outer, core, rim), 64, 1)


def pack_halves(top, bottom, outer):
    return jnp.where(outer, top, bottom) + pltpu.roll(jnp.where(outer, bottom, top), 64, 1)


def fold_all(acc, outer):
    rows = [fold_sublanes([acc[8 * k + i] for i in range(8)]) for k in range(8)]
    return [pack_halves(rows[k], rows[k + 4], outer) for k in range(4)]


def apply_slots(blocks, fields, acc, lead=None):
    step = 16 if blocks.dtype == jnp.bfloat16 else 32
    skip = 0 if lead is None else 1

    def body(ab, carry):
        rows = pl.ds(pl.multiple_of(ab * step, step), step)
        total = jnp.zeros((step, 8, LANES), F32) if lead is None else lead[rows]
        for slot in range(fields.shape[0]):
            for g in range(2):
                piece = blocks[slot + skip, rows, 16 * g : 16 * g + 16, :].astype(F32)
                total = total + piece[:, :8] * fields[slot, 16 * g : 16 * g + 8, :][None]
                total = total + piece[:, 8:] * fields[slot, 16 * g + 8 : 16 * g + 16, :][None]
        acc[rows] = total
        return carry

    lax.fori_loop(0, 64 // step, body, 0)


def apply_one(blocks, parts, outer):
    out = []
    for k in range(8):
        rows = slice(8 * k, 8 * k + 8)
        total = jnp.zeros((8, 8, LANES), F32)
        for g in range(2):
            piece = blocks[rows, 16 * g : 16 * g + 16, :].astype(F32)
            total = total + piece[:, :8] * parts[2 * g][None]
            total = total + piece[:, 8:] * parts[2 * g + 1][None]
        out.append(fold_sublanes([total[i] for i in range(8)]))
    return [pack_halves(out[k], out[k + 4], outer) for k in range(4)]


def home_lanes(is_rim):
    outer = outer_lanes((8, LANES))
    return outer if is_rim else jnp.logical_not(outer)


def lanes_of(columns, slots, is_rim):
    home = home_lanes(is_rim)
    places = [jnp.broadcast_to(columns[s : s + 1, :], (8, LANES)) for s in range(slots)]
    return places, [jnp.where(home, p, p + 64) & (LANES - 1) for p in places]


def gather_inside(columns, slots, is_rim, rim, core, fields, first):
    places, lane = lanes_of(columns, slots, is_rim)
    inner = [((p + 32) & 64) != 0 for p in places]
    for g in range(4):
        part = slice(8 * g, 8 * g + 8)
        for s in range(slots):
            edge = take_lanes(rim[part, :], lane[s])
            middle = take_lanes(core[part, :], lane[s])
            fields[first + s, part, :] = jnp.where(inner[s], middle, edge)


def gather_outside(columns, sent, inside, fields):
    slots = fields.shape[0]
    places, lane = lanes_of(columns, slots, True)
    own = [(p >= 0) & (p < LANES) for p in places]
    for g in range(4):
        part = slice(8 * g, 8 * g + 8)
        left, right = neighbours(*[o[part, :] for o in sent])
        beyond = jnp.where((iota((8, LANES), 1) & 32) == 0, right, left)
        for s in range(slots):
            fields[s, part, :] = jnp.where(own[s], inside[s, part, :], take_lanes(beyond, lane[s]))


def rim_residual(columns, blocks, rhs, inside, lead, sent, fields, acc):
    gather_outside(columns, sent, inside, fields)
    apply_slots(blocks, fields, acc, lead)
    total = fold_all(acc, home_lanes(True))
    return [rhs[8 * g : 8 * g + 8, :] - total[g] for g in range(4)]


def rim_sweep(columns, blocks, inv, rhs, rim, inside, lead, sent, fields, acc):
    res = rim_residual(columns, blocks, rhs, inside, lead, sent, fields, acc)
    step = apply_one(inv, res, home_lanes(True))
    return [rim[8 * g : 8 * g + 8, :] + damping * step[g] for g in range(4)]


def rim_kernel(columns, blocks, inv, rhs, rim, inside, lead, mend, pair, cross, out, fields, acc):
    sent = (mend, pair, cross)
    new = rim_sweep(columns, blocks, inv, rhs, rim, inside, lead, sent, fields, acc)
    for g in range(4):
        out[8 * g : 8 * g + 8, :] = new[g]


def rim_lead(rim, core, rim_columns, rim_blocks, inside, lead):
    gather_inside(rim_columns, inside.shape[0], True, rim, core, inside, 0)
    for k in range(8):
        rows = slice(8 * k, 8 * k + 8)
        total = rim_blocks[0, rows, 0:8, :] * rim[0:8, :][None]
        for g in range(1, 4):
            part = slice(8 * g, 8 * g + 8)
            total = total + rim_blocks[0, rows, part, :] * rim[part, :][None]
        lead[rows] = total


def lead_kernel(rim, core, rim_columns, rim_blocks, inside, lead):
    rim_lead(rim, core, rim_columns, rim_blocks, inside, lead)


def core_residual(columns, blocks, rhs, rim, core, fields, acc):
    fields[0] = core[...]
    gather_inside(columns, fields.shape[0] - 1, False, rim, core, fields, 1)
    apply_slots(blocks, fields, acc)
    total = fold_all(acc, home_lanes(False))
    return [rhs[8 * g : 8 * g + 8, :] - total[g] for g in range(4)]


def core_alone_kernel(columns, blocks, rhs, rim, core, inv, out, fields, acc):
    step = apply_one(inv, core_residual(columns, blocks, rhs, rim, core, fields, acc), home_lanes(False))
    for g in range(4):
        part = slice(8 * g, 8 * g + 8)
        out[part, :] = core[part, :] + damping * step[g]


def core_kernel(
    columns, blocks, rhs, rim, core, rim_columns, rim_blocks, inv, out, inside, lead, fields, acc
):
    rim_lead(rim, core, rim_columns, rim_blocks, inside, lead)
    res = core_residual(columns, blocks, rhs, rim, core, fields, acc)
    step = apply_one(inv, res, home_lanes(False))
    for g in range(4):
        part = slice(8 * g, 8 * g + 8)
        out[part, :] = core[part, :] + damping * step[g]


def core_residual_kernel(
    columns, blocks, rhs, rim, core, rim_columns, rim_blocks, out, inside, lead, fields, acc
):
    rim_lead(rim, core, rim_columns, rim_blocks, inside, lead)
    res = core_residual(columns, blocks, rhs, rim, core, fields, acc)
    for g in range(4):
        out[8 * g : 8 * g + 8, :] = res[g]


def last_kernel(
    columns, blocks, inv, rhs, rim, inside, lead, mend, pair, cross, new_core,
    out, fields, acc, held, sem,
):
    sent = (mend, pair, cross)
    new = rim_sweep(columns, blocks, inv, rhs, rim, inside, lead, sent, fields, acc)
    for g in range(4):
        part = slice(8 * g, 8 * g + 8)
        top, bottom = join_field(new[g], new_core[part, :])
        held[part, :] = top
        held[32 + 8 * g : 40 + 8 * g, :] = bottom
    copy = pltpu.make_async_copy(held, out, sem)
    copy.start()
    copy.wait()


def first_kernel(
    inv, rhs, columns, agg, ccolumns,
    rim, core, rim_inv, core_inv, rim_rhs, core_rhs, rim_columns, core_columns, near,
    held, rhs_in, col_in, agg_in, ccol_in, sems,
):
    device, _ = place_on_line()
    copies = [pltpu.make_async_copy(rhs, rhs_in, sems.at[8])] + [
        pltpu.make_async_copy(inv.at[pl.ds(8 * k, 8)], held.at[pl.ds(8 * k, 8)], sems.at[k])
        for k in range(8)
    ]
    small = [
        pltpu.make_async_copy(columns, col_in, sems.at[9]),
        pltpu.make_async_copy(agg, agg_in, sems.at[10]),
        pltpu.make_async_copy(ccolumns, ccol_in, sems.at[11]),
    ]
    for copy in copies + small:
        copy.start()
    copies[0].wait()
    own = ([], [])
    for g in range(4):
        part = slice(8 * g, 8 * g + 8)
        edge, middle = split_field(rhs_in[part, :], rhs_in[32 + 8 * g : 40 + 8 * g, :])
        rim_rhs[part, :] = edge
        core_rhs[part, :] = middle
        own[0].append(edge)
        own[1].append(middle)
    sums = ([], [])
    for k in range(8):
        copies[k + 1].wait()
        rows = slice(8 * k, 8 * k + 8)
        both = split_field(held[rows, :32, :], held[rows, 32:, :])
        core_inv[rows] = both[1]
        both = [piece.astype(F32) for piece in both]
        rim_inv[rows] = both[0]
        for piece, parts, kept in zip(both, own, sums):
            total = piece[:, 0:8] * parts[0][None]
            for g in range(1, 4):
                total = total + piece[:, 8 * g : 8 * g + 8] * parts[g][None]
            kept.append(fold_sublanes([total[i] for i in range(8)]))
    for out, kept, home in ((rim, sums[0], True), (core, sums[1], False)):
        for g in range(4):
            total = pack_halves(kept[g], kept[g + 4], home_lanes(home))
            out[8 * g : 8 * g + 8, :] = damping * total
    for copy in small:
        copy.wait()
    slots = columns.shape[0]
    rows = iota((8, LANES), 0)
    table = jnp.broadcast_to(agg_in[...], (8, LANES))
    for s in range(slots):
        table = jnp.where(
            rows == s, jnp.broadcast_to(col_in[s : s + 1, :] - device * LANES, (8, LANES)), table
        )
    turned = pltpu.roll(table, 64, 1)
    outer = outer_lanes((8, LANES))
    rim_columns[...] = jnp.where(outer, table, turned)
    core_columns[...] = jnp.where(outer, turned, table)
    count = ccol_in.shape[1]
    tiled = jnp.concatenate([ccol_in[...]] * (LANES // count), axis=1)
    chosen = jnp.where(rows == iota((8, LANES), 1) // count, tiled - device * count, 0)
    near[...] = jnp.broadcast_to(jnp.sum(chosen, axis=0, keepdims=True), (8, LANES))


def widen_kernel(diag, off, rim_out, core_out, held, sems):
    slots = off.shape[0] + 1
    parts, ahead = 4, 14
    each = diag.shape[0] // parts
    copies = []
    for s in range(slots):
        src = diag if s == 0 else off.at[s - 1]
        for k in range(parts):
            rows = pl.ds(each * k, each)
            copies.append(pltpu.make_async_copy(src.at[rows], held.at[s, rows], sems.at[s, k]))
    for copy in copies[:ahead]:
        copy.start()
    for i, copy in enumerate(copies):
        copy.wait()
        if i + ahead < len(copies):
            copies[i + ahead].start()
        s, k = divmod(i, parts)
        rows = pl.ds(each * k, each)
        rim, core = split_field(held[s, rows, :32, :], held[s, rows, 32:, :])
        rim_out[s, rows] = rim.astype(F32)
        core_out[s, rows] = core


def turn(block):
    return jnp.transpose(block.astype(F32), (1, 0))


def coarse_ends_kernel(diag, inv, diag_out, inv_out):
    for src, dst in ((inv, inv_out), (diag, diag_out)):
        for r in range(8):
            dst[r] = turn(jnp.concatenate([src[8 * h + r] for h in range(8)], axis=0))


def coarse_off_kernel(off, off_out):
    slots, size = off.shape[:2]

    def body(i, carry):
        for j in range(8):
            a = 8 * i + j
            off_out[a] = turn(jnp.concatenate([off[s, a] for s in range(slots)], axis=0))
        return carry

    lax.fori_loop(0, size // 8, body, 0)


def pack_rows(full):
    group = iota((8, LANES), 1) // 16
    out = full[0:8, :]
    for g in range(1, 8):
        out = jnp.where(group == g, full[8 * g : 8 * g + 8, :], out)
    return out


def spread_rows(packed):
    lane = iota((8, LANES), 1) & 15
    return [take_lanes(packed, lane + 16 * h) for h in range(8)]


def small_apply(blocks, fields):
    parts = []
    for r in range(8):
        acc = blocks[r, 0:8, :] * fields[0]
        for g in range(1, 8):
            acc = acc + blocks[r, 8 * g : 8 * g + 8, :] * fields[g]
        parts.append(acc)
    return fold_sublanes(parts)


def coarse_off_apply(off, fields):
    parts = []
    for ab in range(8):
        rows = slice(8 * ab, 8 * ab + 8)
        acc = off[rows, 0:8, :] * fields[0][None]
        for g in range(1, 8):
            acc = acc + off[rows, 8 * g : 8 * g + 8, :] * fields[g][None]
        total = fold_sublanes([acc[i] for i in range(8)])
        for shift in (64, 32, 16):
            total = total + pltpu.roll(total, shift, 1)
        parts.append(total)
    return parts


def restrict_kernel(
    columns, blocks, rhs, core_res, inside, lead, mend, pair, cross, core_columns, cinv,
    coarse_rhs, out, fields, acc,
):
    res = rim_residual(columns, blocks, rhs, inside, lead, (mend, pair, cross), fields, acc)
    inner = core_res[...]
    edge = jnp.concatenate(res, axis=0)
    r = jnp.concatenate(join_field(edge, inner), axis=0)
    hi = r.astype(jnp.bfloat16)
    rest = r - hi.astype(F32)
    mid = rest.astype(jnp.bfloat16)
    last = (rest - mid.astype(F32)).astype(jnp.bfloat16)
    parts = jnp.concatenate([hi, mid, last], axis=0)
    slots = fields.shape[0]
    agg = jnp.where(
        outer_lanes((1, LANES)), columns[slots : slots + 1, :], core_columns[slots : slots + 1, :]
    )
    row_of = jnp.broadcast_to(agg, (LANES, LANES))
    select = jnp.where(row_of == (iota((LANES, LANES), 0) & 15), 1.0, 0.0).astype(jnp.bfloat16)
    sums = lax.dot_general(parts, select, (((1,), (1,)), ((), ())), preferred_element_type=F32)
    full = sums[0:64] + (sums[64:128] + sums[128:192])
    coarse_rhs[...] = pack_rows(full)
    out[...] = damping * small_apply(cinv, [full[8 * g : 8 * g + 8] for g in range(8)])


def coarse_step(places, cdiag, coff, cinv, coarse_rhs, u, mend, pair, cross):
    left, right = neighbours(mend[...], pair[...], cross[...])
    places = places[...]
    inner = places & 15
    mine = u[...]
    fields = []
    for g in range(8):
        lane = inner + 16 * g
        fields.append(
            jnp.where(
                places < 0,
                take_lanes(left, lane),
                jnp.where(places < 16, take_lanes(mine, lane), take_lanes(right, lane)),
            )
        )
    base = spread_rows(coarse_rhs[...] - small_apply(cdiag, spread_rows(mine)))
    total = coarse_off_apply(coff, fields)
    return mine + damping * small_apply(cinv, [a - b for a, b in zip(base, total)])


def coarse_kernel(places, cdiag, coff, cinv, coarse_rhs, u, mend, pair, cross, out):
    out[...] = coarse_step(places, cdiag, coff, cinv, coarse_rhs, u, mend, pair, cross)


def prolong_kernel(
    places, cdiag, coff, cinv, coarse_rhs, u, mend, pair, cross, rim_columns, core_columns, rim, core,
    rim_out, core_out,
):
    last = coarse_step(places, cdiag, coff, cinv, coarse_rhs, u, mend, pair, cross)
    row = 6
    tables = ((rim_columns, rim, rim_out, True), (core_columns, core, core_out, False))
    for table, old, out, is_rim in tables:
        lane = jnp.broadcast_to(table[row : row + 1, :], (8, LANES))
        lane = jnp.where(home_lanes(is_rim), lane, lane + 64)
        for g in range(4):
            part = slice(8 * g, 8 * g + 8)
            out[part, :] = old[part, :] + take_lanes(last, lane + 16 * g)


def in_vmem(array):
    return pltpu.with_memory_space_constraint(array, pltpu.VMEM)


VM = pl.BlockSpec(memory_space=pltpu.VMEM)
FAR = pl.BlockSpec(memory_space=pltpu.HBM)


def call(kernel, outs, args, scratch=(), far=False, limit=4, flops=0, moved=0):
    shapes = [pltpu.VMEM(o[0], o[1]) if isinstance(o[0], tuple) else pltpu.VMEM(o, F32) for o in outs]
    place = pltpu.HBM if far else pltpu.VMEM
    return pl.pallas_call(
        kernel,
        out_shape=shapes if len(shapes) > 1 else shapes[0],
        in_specs=[pl.BlockSpec(memory_space=place)] * len(args),
        out_specs=[VM] * len(shapes) if len(shapes) > 1 else VM,
        scratch_shapes=list(scratch),
        compiler_params=pltpu.CompilerParams(vmem_limit_bytes=limit * 1024 * 1024),
    )(*[pltpu.with_memory_space_constraint(a, place) for a in args])


def shards(
    right_side,
    fine_diag,
    fine_off,
    fine_inv,
    fine_columns,
    aggregate,
    coarse_diag,
    coarse_off,
    coarse_inv,
    coarse_columns,
):
    size, rows = right_side.shape
    slots = fine_off.shape[0]
    own_rows = coarse_diag.shape[2]
    ways = routes(lax.axis_size(AXES))
    bf16 = jnp.bfloat16
    i32 = jnp.int32
    full = (size, rows)
    half = (size // 2, rows)
    packed = (8, LANES)
    table = ((8, LANES), i32)
    blocks = (slots + 1, size, size // 2, rows)
    turned = (8, size, LANES)
    sem = pltpu.SemaphoreType.DMA
    work = [pltpu.VMEM((slots + 1,) + half, F32), pltpu.VMEM((size, 8, LANES), F32)]

    rim, core, rim_inv, core_inv, rim_rhs, core_rhs, rim_cols, core_cols, near = call(
        first_kernel,
        [half, half, blocks[1:], (blocks[1:], bf16), half, half, table, table, table],
        [fine_inv, right_side, fine_columns, aggregate.reshape(1, rows), coarse_columns],
        [
            pltpu.VMEM(fine_inv.shape, bf16),
            pltpu.VMEM(full, F32),
            pltpu.VMEM((slots, rows), i32),
            pltpu.VMEM((1, rows), i32),
            pltpu.VMEM(coarse_columns.shape, i32),
            sem((12,)),
        ],
        far=True,
    )
    rim_blocks, core_blocks = call(
        widen_kernel,
        [blocks, (blocks, bf16)],
        [fine_diag, fine_off],
        [pltpu.VMEM((slots + 1, size, size, rows), bf16), sem((slots + 1, 4))],
        far=True,
        limit=12,
    )
    ends = [jnp.transpose(coarse_diag, (0, 2, 1)), jnp.transpose(coarse_inv, (0, 2, 1))]
    cdiag, cinv = call(coarse_ends_kernel, [turned, turned], ends)
    others = jnp.transpose(coarse_off, (0, 1, 3, 2))
    coff = call(coarse_off_kernel, [(size, size, LANES)], [others])

    rim_work = [pltpu.VMEM((slots,) + half, F32), work[1]]
    ready = [half, (slots,) + half, (size, 8, LANES)]

    def core_args(rim, core):
        return [core_cols, core_blocks, core_rhs, rim, core, rim_cols, rim_blocks]

    def sweep_core(rim, core):
        return call(core_kernel, ready, core_args(rim, core) + [core_inv], work)

    def rim_args(rim, inside, lead, sent):
        return [rim_cols, rim_blocks, rim_inv, rim_rhs, rim, inside, lead, *sent]

    def sweep(rim, core):
        sent = exchange(rim, ways)
        core, inside, lead = sweep_core(rim, core)
        return call(rim_kernel, [half], rim_args(rim, inside, lead, sent), rim_work), core

    for cycle in range(CYCLES):
        for step in range(SWEEPS):
            if cycle:
                rim, core = sweep(rim, core)
            elif step:
                sent = exchange(rim, ways)
                inside, lead = call(lead_kernel, ready[1:], [rim, core, rim_cols, rim_blocks])
                args = [core_cols, core_blocks, core_rhs, rim, core, core_inv]
                new_core = call(core_alone_kernel, [half], args, work)
                rim = call(rim_kernel, [half], rim_args(rim, inside, lead, sent), rim_work)
                core = new_core
        sent = exchange(rim, ways)
        core_res, inside, lead = call(core_residual_kernel, ready, core_args(rim, core), work)
        crhs, u = call(
            restrict_kernel,
            [packed, packed],
            [rim_cols, rim_blocks, rim_rhs, core_res, inside, lead, *sent, core_cols, cinv],
            rim_work,
        )
        for step in range(1, CSWEEPS):
            base = [near, cdiag, coff, cinv, crhs, u, *exchange(u, ways)]
            if step < CSWEEPS - 1:
                u = call(coarse_kernel, [packed], base)
            else:
                rim, core = call(prolong_kernel, [half, half], base + [rim_cols, core_cols, rim, core])
        for step in range(SWEEPS - (cycle == CYCLES - 1)):
            rim, core = sweep(rim, core)
    sent = exchange(rim, ways)
    core, inside, lead = sweep_core(rim, core)
    args = rim_args(rim, inside, lead, sent) + [core]
    return pl.pallas_call(
        last_kernel,
        out_shape=pltpu.HBM(full, F32),
        in_specs=[VM] * len(args),
        out_specs=FAR,
        scratch_shapes=rim_work + [pltpu.VMEM(full, F32), sem(())],
        compiler_params=pltpu.CompilerParams(vmem_limit_bytes=4 * 1024 * 1024),
    )(*[in_vmem(a) for a in args])


def solution(mesh):
    placed = (
        P(None, AXES),
        P(None, None, AXES),
        P(None, None, None, AXES),
        P(None, None, AXES),
        P(None, AXES),
        P(AXES),
        P(None, None, AXES),
        P(None, None, None, AXES),
        P(None, None, AXES),
        P(None, AXES),
    )
    return jax.shard_map(
        shards, mesh=mesh, in_specs=placed, out_specs=P(None, AXES), check_vma=False
    )
```

```python
import jax
import jax.numpy as jnp
from jax import lax
from jax.experimental import pallas as pl
from jax.experimental.pallas import tpu as pltpu
from jax.sharding import PartitionSpec as P

SWEEPS = 2
CSWEEPS = 4
CYCLES = 2
AXES = ("brick", "group")
LINE = 4

damping = 0.7
LANES = 128
F32 = jnp.float32


def routes(count):
    last = count - 1
    cross = []
    for i in range(3, last, 2):
        if i + 1 < last - 1:
            cross += [(i, i + 1), (i + 1, i)]
    cross += [(0, 1), (1, 2), (2, 0), (last - 2, last - 1), (last - 1, last), (last, last - 2)]
    pair = [(i, i ^ 1) for i in range(count)]
    mend = []
    for i in range(count):
        spot = i % LINE
        if spot in (0, LINE - 1):
            mend.append((i, i ^ LINE))
        else:
            low = (i // LINE) % LINE in (0, LINE - 1)
            back = spot == 2
            mend.append((i, i - 1 if low and back else i + 1 if not low and not back else i ^ LINE))
    for way in (mend, pair, cross):
        assert sorted(t for _, t in way) == sorted(f for f, _ in way) == list(range(count))
    return mend, pair, cross


def exchange(field, ways):
    return [lax.ppermute(field, AXES, way) for way in ways]


def iota(shape, dim):
    return lax.broadcasted_iota(jnp.int32, shape, dim)


def fold_sublanes(parts):
    rows = iota(parts[0].shape, 0)
    shift = 4
    while shift:
        low = (rows & shift) == 0
        parts = [
            jnp.where(low, a, b) + pltpu.roll(jnp.where(low, b, a), 4 if shift == 4 else (8 - shift), 0)
            if shift == 4
            else fold_pair(a, b, low, shift, 0)
            for a, b in zip(parts[:shift], parts[shift:])
        ]
        shift //= 2
    return parts[0]


def fold_pair(a, b, low, shift, axis):
    size = a.shape[axis]
    own = jnp.where(low, a, b)
    other = jnp.where(low, b, a)
    return own + jnp.where(
        low, pltpu.roll(other, size - shift, axis), pltpu.roll(other, shift, axis)
    )


def take_lanes(field, places):
    return jnp.take_along_axis(field, places, axis=1, mode="promise_in_bounds")


def place_on_line():
    return lax.axis_index(AXES), lax.axis_size(AXES)


def neighbours(mend, pair, cross):
    device, count = place_on_line()
    even = lax.rem(device, 2) == 0
    ends = (device == 1) | (device == count - 3)
    left = jnp.where(even, cross, pair)
    right = jnp.where(even, pair, jnp.where(ends, mend, cross))
    left = jnp.where(device == 0, 0.0, left)
    right = jnp.where(device == count - 1, 0.0, right)
    return left, right


def outer_lanes(shape):
    lanes = iota(shape, len(shape) - 1)
    return (lanes < 32) | (lanes >= 96)


def split_field(top, bottom):
    outer = outer_lanes(top.shape)
    turned = pltpu.roll(bottom, 64, top.ndim - 1)
    return jnp.where(outer, top, turned), jnp.where(outer, turned, top)


def join_field(rim, core):
    outer = outer_lanes(rim.shape)
    return jnp.where(outer, rim, core), pltpu.roll(jnp.where(outer, core, rim), 64, 1)


def pack_halves(top, bottom, outer):
    return jnp.where(outer, top, bottom) + pltpu.roll(jnp.where(outer, bottom, top), 64, 1)


def fold_all(acc, outer):
    rows = [fold_sublanes([acc[8 * k + i] for i in range(8)]) for k in range(8)]
    return [pack_halves(rows[k], rows[k + 4], outer) for k in range(4)]


def apply_slots(blocks, fields, acc, lead=None):
    step = 16 if blocks.dtype == jnp.bfloat16 else 32
    skip = 0 if lead is None else 1

    def body(ab, carry):
        rows = pl.ds(pl.multiple_of(ab * step, step), step)
        total = jnp.zeros((step, 8, LANES), F32) if lead is None else lead[rows]
        for slot in range(fields.shape[0]):
            for g in range(2):
                piece = blocks[slot + skip, rows, 16 * g : 16 * g + 16, :].astype(F32)
                total = total + piece[:, :8] * fields[slot, 16 * g : 16 * g + 8, :][None]
                total = total + piece[:, 8:] * fields[slot, 16 * g + 8 : 16 * g + 16, :][None]
        acc[rows] = total
        return carry

    lax.fori_loop(0, 64 // step, body, 0)


def apply_one(blocks, parts, outer):
    out = []
    for k in range(8):
        rows = slice(8 * k, 8 * k + 8)
        total = jnp.zeros((8, 8, LANES), F32)
        for g in range(2):
            piece = blocks[rows, 16 * g : 16 * g + 16, :].astype(F32)
            total = total + piece[:, :8] * parts[2 * g][None]
            total = total + piece[:, 8:] * parts[2 * g + 1][None]
        out.append(fold_sublanes([total[i] for i in range(8)]))
    return [pack_halves(out[k], out[k + 4], outer) for k in range(4)]


def home_lanes(is_rim):
    outer = outer_lanes((8, LANES))
    return outer if is_rim else jnp.logical_not(outer)


def lanes_of(columns, slots, is_rim):
    home = home_lanes(is_rim)
    places = [jnp.broadcast_to(columns[s : s + 1, :], (8, LANES)) for s in range(slots)]
    return places, [jnp.where(home, p, p + 64) & (LANES - 1) for p in places]


def gather_inside(columns, slots, is_rim, rim, core, fields, first):
    places, lane = lanes_of(columns, slots, is_rim)
    inner = [((p + 32) & 64) != 0 for p in places]
    for g in range(4):
        part = slice(8 * g, 8 * g + 8)
        for s in range(slots):
            edge = take_lanes(rim[part, :], lane[s])
            middle = take_lanes(core[part, :], lane[s])
            fields[first + s, part, :] = jnp.where(inner[s], middle, edge)


def gather_outside(columns, sent, inside, fields):
    slots = fields.shape[0]
    places, lane = lanes_of(columns, slots, True)
    own = [(p >= 0) & (p < LANES) for p in places]
    for g in range(4):
        part = slice(8 * g, 8 * g + 8)
        left, right = neighbours(*[o[part, :] for o in sent])
        beyond = jnp.where((iota((8, LANES), 1) & 32) == 0, right, left)
        for s in range(slots):
            fields[s, part, :] = jnp.where(own[s], inside[s, part, :], take_lanes(beyond, lane[s]))


def rim_residual(columns, blocks, rhs, inside, lead, sent, fields, acc):
    gather_outside(columns, sent, inside, fields)
    apply_slots(blocks, fields, acc, lead)
    total = fold_all(acc, home_lanes(True))
    return [rhs[8 * g : 8 * g + 8, :] - total[g] for g in range(4)]


def rim_sweep(columns, blocks, inv, rhs, rim, inside, lead, sent, fields, acc):
    res = rim_residual(columns, blocks, rhs, inside, lead, sent, fields, acc)
    step = apply_one(inv, res, home_lanes(True))
    return [rim[8 * g : 8 * g + 8, :] + damping * step[g] for g in range(4)]


def rim_kernel(columns, blocks, inv, rhs, rim, inside, lead, mend, pair, cross, out, fields, acc):
    sent = (mend, pair, cross)
    new = rim_sweep(columns, blocks, inv, rhs, rim, inside, lead, sent, fields, acc)
    for g in range(4):
        out[8 * g : 8 * g + 8, :] = new[g]


def rim_lead(rim, core, rim_columns, rim_blocks, inside, lead):
    gather_inside(rim_columns, inside.shape[0], True, rim, core, inside, 0)
    for k in range(8):
        rows = slice(8 * k, 8 * k + 8)
        total = rim_blocks[0, rows, 0:8, :] * rim[0:8, :][None]
        for g in range(1, 4):
            part = slice(8 * g, 8 * g + 8)
            total = total + rim_blocks[0, rows, part, :] * rim[part, :][None]
        lead[rows] = total


def lead_kernel(rim, core, rim_columns, rim_blocks, inside, lead):
    rim_lead(rim, core, rim_columns, rim_blocks, inside, lead)


def core_residual(columns, blocks, rhs, rim, core, fields, acc):
    fields[0] = core[...]
    gather_inside(columns, fields.shape[0] - 1, False, rim, core, fields, 1)
    apply_slots(blocks, fields, acc)
    total = fold_all(acc, home_lanes(False))
    return [rhs[8 * g : 8 * g + 8, :] - total[g] for g in range(4)]


def core_alone_kernel(columns, blocks, rhs, rim, core, inv, out, fields, acc):
    step = apply_one(inv, core_residual(columns, blocks, rhs, rim, core, fields, acc), home_lanes(False))
    for g in range(4):
        part = slice(8 * g, 8 * g + 8)
        out[part, :] = core[part, :] + damping * step[g]


def core_kernel(
    columns, blocks, rhs, rim, core, rim_columns, rim_blocks, inv, out, inside, lead, fields, acc
):
    rim_lead(rim, core, rim_columns, rim_blocks, inside, lead)
    res = core_residual(columns, blocks, rhs, rim, core, fields, acc)
    step = apply_one(inv, res, home_lanes(False))
    for g in range(4):
        part = slice(8 * g, 8 * g + 8)
        out[part, :] = core[part, :] + damping * step[g]


def core_residual_kernel(
    columns, blocks, rhs, rim, core, rim_columns, rim_blocks, out, inside, lead, fields, acc
):
    rim_lead(rim, core, rim_columns, rim_blocks, inside, lead)
    res = core_residual(columns, blocks, rhs, rim, core, fields, acc)
    for g in range(4):
        out[8 * g : 8 * g + 8, :] = res[g]


def last_kernel(
    columns, blocks, inv, rhs, rim, inside, lead, mend, pair, cross, new_core,
    out, fields, acc, held, sems,
):
    sent = (mend, pair, cross)
    new = rim_sweep(columns, blocks, inv, rhs, rim, inside, lead, sent, fields, acc)
    copies = []
    for g in range(4):
        part = slice(8 * g, 8 * g + 8)
        top, bottom = join_field(new[g], new_core[part, :])
        held[part, :] = top
        below = slice(32 + 8 * g, 40 + 8 * g)
        held[below, :] = bottom
        for i, rows in enumerate((part, below)):
            copies.append(pltpu.make_async_copy(held.at[rows], out.at[rows], sems.at[g, i]))
            copies[-1].start()
    for copy in copies:
        copy.wait()


def first_kernel(
    inv, rhs, columns, agg, ccolumns,
    rim, core, rim_inv, core_inv, rim_rhs, core_rhs, rim_columns, core_columns, near,
    held, rhs_in, col_in, agg_in, ccol_in, sems,
):
    device, _ = place_on_line()
    copies = [pltpu.make_async_copy(rhs, rhs_in, sems.at[8])] + [
        pltpu.make_async_copy(inv.at[pl.ds(8 * k, 8)], held.at[pl.ds(8 * k, 8)], sems.at[k])
        for k in range(8)
    ]
    small = [
        pltpu.make_async_copy(columns, col_in, sems.at[9]),
        pltpu.make_async_copy(agg, agg_in, sems.at[10]),
        pltpu.make_async_copy(ccolumns, ccol_in, sems.at[11]),
    ]
    for copy in copies + small:
        copy.start()
    copies[0].wait()
    own = ([], [])
    for g in range(4):
        part = slice(8 * g, 8 * g + 8)
        edge, middle = split_field(rhs_in[part, :], rhs_in[32 + 8 * g : 40 + 8 * g, :])
        rim_rhs[part, :] = edge
        core_rhs[part, :] = middle
        own[0].append(edge)
        own[1].append(middle)
    sums = ([], [])
    for k in range(8):
        copies[k + 1].wait()
        rows = slice(8 * k, 8 * k + 8)
        both = split_field(held[rows, :32, :], held[rows, 32:, :])
        core_inv[rows] = both[1]
        both = [piece.astype(F32) for piece in both]
        rim_inv[rows] = both[0]
        for piece, parts, kept in zip(both, own, sums):
            total = piece[:, 0:8] * parts[0][None]
            for g in range(1, 4):
                total = total + piece[:, 8 * g : 8 * g + 8] * parts[g][None]
            kept.append(fold_sublanes([total[i] for i in range(8)]))
    for out, kept, home in ((rim, sums[0], True), (core, sums[1], False)):
        for g in range(4):
            total = pack_halves(kept[g], kept[g + 4], home_lanes(home))
            out[8 * g : 8 * g + 8, :] = damping * total
    for copy in small:
        copy.wait()
    slots = columns.shape[0]
    rows = iota((8, LANES), 0)
    table = jnp.broadcast_to(agg_in[...], (8, LANES))
    for s in range(slots):
        table = jnp.where(
            rows == s, jnp.broadcast_to(col_in[s : s + 1, :] - device * LANES, (8, LANES)), table
        )
    turned = pltpu.roll(table, 64, 1)
    outer = outer_lanes((8, LANES))
    rim_columns[...] = jnp.where(outer, table, turned)
    core_columns[...] = jnp.where(outer, turned, table)
    count = ccol_in.shape[1]
    tiled = jnp.concatenate([ccol_in[...]] * (LANES // count), axis=1)
    chosen = jnp.where(rows == iota((8, LANES), 1) // count, tiled - device * count, 0)
    near[...] = jnp.broadcast_to(jnp.sum(chosen, axis=0, keepdims=True), (8, LANES))


def widen_kernel(diag, off, rim_out, core_out, held, sems):
    slots = off.shape[0] + 1
    parts, ahead = 4, 22
    each = diag.shape[0] // parts
    copies = []
    for s in range(slots):
        src = diag if s == 0 else off.at[s - 1]
        for k in range(parts):
            rows = pl.ds(each * k, each)
            copies.append(pltpu.make_async_copy(src.at[rows], held.at[s, rows], sems.at[s, k]))
    for copy in copies[:ahead]:
        copy.start()
    for i, copy in enumerate(copies):
        copy.wait()
        if i + ahead < len(copies):
            copies[i + ahead].start()
        s, k = divmod(i, parts)
        rows = pl.ds(each * k, each)
        rim, core = split_field(held[s, rows, :32, :], held[s, rows, 32:, :])
        rim_out[s, rows] = rim.astype(F32)
        core_out[s, rows] = core


def turn(block):
    return jnp.transpose(block.astype(F32), (1, 0))


def coarse_ends_kernel(diag, inv, diag_out, inv_out):
    for src, dst in ((inv, inv_out), (diag, diag_out)):
        for r in range(8):
            dst[r] = turn(jnp.concatenate([src[8 * h + r] for h in range(8)], axis=0))


def coarse_off_kernel(off, off_out):
    slots, size = off.shape[:2]

    def body(i, carry):
        for j in range(8):
            a = 8 * i + j
            off_out[a] = turn(jnp.concatenate([off[s, a] for s in range(slots)], axis=0))
        return carry

    lax.fori_loop(0, size // 8, body, 0)


def pack_rows(full):
    group = iota((8, LANES), 1) // 16
    out = full[0:8, :]
    for g in range(1, 8):
        out = jnp.where(group == g, full[8 * g : 8 * g + 8, :], out)
    return out


def spread_rows(packed):
    lane = iota((8, LANES), 1) & 15
    return [take_lanes(packed, lane + 16 * h) for h in range(8)]


def small_apply(blocks, fields):
    parts = []
    for r in range(8):
        acc = blocks[r, 0:8, :] * fields[0]
        for g in range(1, 8):
            acc = acc + blocks[r, 8 * g : 8 * g + 8, :] * fields[g]
        parts.append(acc)
    return fold_sublanes(parts)


def coarse_off_apply(off, fields):
    parts = []
    for ab in range(8):
        rows = slice(8 * ab, 8 * ab + 8)
        acc = off[rows, 0:8, :] * fields[0][None]
        for g in range(1, 8):
            acc = acc + off[rows, 8 * g : 8 * g + 8, :] * fields[g][None]
        total = fold_sublanes([acc[i] for i in range(8)])
        for shift in (64, 32, 16):
            total = total + pltpu.roll(total, shift, 1)
        parts.append(total)
    return parts


def restrict_kernel(
    columns, blocks, rhs, core_res, inside, lead, mend, pair, cross, core_columns, cinv,
    coarse_rhs, out, fields, acc,
):
    res = rim_residual(columns, blocks, rhs, inside, lead, (mend, pair, cross), fields, acc)
    inner = core_res[...]
    edge = jnp.concatenate(res, axis=0)
    r = jnp.concatenate(join_field(edge, inner), axis=0)
    hi = r.astype(jnp.bfloat16)
    rest = r - hi.astype(F32)
    mid = rest.astype(jnp.bfloat16)
    last = (rest - mid.astype(F32)).astype(jnp.bfloat16)
    parts = jnp.concatenate([hi, mid, last], axis=0)
    slots = fields.shape[0]
    agg = jnp.where(
        outer_lanes((1, LANES)), columns[slots : slots + 1, :], core_columns[slots : slots + 1, :]
    )
    row_of = jnp.broadcast_to(agg, (LANES, LANES))
    select = jnp.where(row_of == (iota((LANES, LANES), 0) & 15), 1.0, 0.0).astype(jnp.bfloat16)
    sums = lax.dot_general(parts, select, (((1,), (1,)), ((), ())), preferred_element_type=F32)
    full = sums[0:64] + (sums[64:128] + sums[128:192])
    coarse_rhs[...] = pack_rows(full)
    out[...] = damping * small_apply(cinv, [full[8 * g : 8 * g + 8] for g in range(8)])


def coarse_step(places, cdiag, coff, cinv, coarse_rhs, u, mend, pair, cross):
    left, right = neighbours(mend[...], pair[...], cross[...])
    places = places[...]
    inner = places & 15
    mine = u[...]
    fields = []
    for g in range(8):
        lane = inner + 16 * g
        fields.append(
            jnp.where(
                places < 0,
                take_lanes(left, lane),
                jnp.where(places < 16, take_lanes(mine, lane), take_lanes(right, lane)),
            )
        )
    base = spread_rows(coarse_rhs[...] - small_apply(cdiag, spread_rows(mine)))
    total = coarse_off_apply(coff, fields)
    return mine + damping * small_apply(cinv, [a - b for a, b in zip(base, total)])


def coarse_kernel(places, cdiag, coff, cinv, coarse_rhs, u, mend, pair, cross, out):
    out[...] = coarse_step(places, cdiag, coff, cinv, coarse_rhs, u, mend, pair, cross)


def prolong_kernel(
    places, cdiag, coff, cinv, coarse_rhs, u, mend, pair, cross, rim_columns, core_columns, rim, core,
    rim_out, core_out,
):
    last = coarse_step(places, cdiag, coff, cinv, coarse_rhs, u, mend, pair, cross)
    row = 6
    tables = ((rim_columns, rim, rim_out, True), (core_columns, core, core_out, False))
    for table, old, out, is_rim in tables:
        lane = jnp.broadcast_to(table[row : row + 1, :], (8, LANES))
        lane = jnp.where(home_lanes(is_rim), lane, lane + 64)
        for g in range(4):
            part = slice(8 * g, 8 * g + 8)
            out[part, :] = old[part, :] + take_lanes(last, lane + 16 * g)


def in_vmem(array):
    return pltpu.with_memory_space_constraint(array, pltpu.VMEM)


VM = pl.BlockSpec(memory_space=pltpu.VMEM)
FAR = pl.BlockSpec(memory_space=pltpu.HBM)


def call(kernel, outs, args, scratch=(), far=False, limit=4, flops=0, moved=0):
    shapes = [pltpu.VMEM(o[0], o[1]) if isinstance(o[0], tuple) else pltpu.VMEM(o, F32) for o in outs]
    place = pltpu.HBM if far else pltpu.VMEM
    return pl.pallas_call(
        kernel,
        out_shape=shapes if len(shapes) > 1 else shapes[0],
        in_specs=[pl.BlockSpec(memory_space=place)] * len(args),
        out_specs=[VM] * len(shapes) if len(shapes) > 1 else VM,
        scratch_shapes=list(scratch),
        compiler_params=pltpu.CompilerParams(vmem_limit_bytes=limit * 1024 * 1024),
    )(*[pltpu.with_memory_space_constraint(a, place) for a in args])


def shards(
    right_side,
    fine_diag,
    fine_off,
    fine_inv,
    fine_columns,
    aggregate,
    coarse_diag,
    coarse_off,
    coarse_inv,
    coarse_columns,
):
    size, rows = right_side.shape
    slots = fine_off.shape[0]
    own_rows = coarse_diag.shape[2]
    ways = routes(lax.axis_size(AXES))
    bf16 = jnp.bfloat16
    i32 = jnp.int32
    full = (size, rows)
    half = (size // 2, rows)
    packed = (8, LANES)
    table = ((8, LANES), i32)
    blocks = (slots + 1, size, size // 2, rows)
    turned = (8, size, LANES)
    sem = pltpu.SemaphoreType.DMA
    work = [pltpu.VMEM((slots + 1,) + half, F32), pltpu.VMEM((size, 8, LANES), F32)]

    rim, core, rim_inv, core_inv, rim_rhs, core_rhs, rim_cols, core_cols, near = call(
        first_kernel,
        [half, half, blocks[1:], (blocks[1:], bf16), half, half, table, table, table],
        [fine_inv, right_side, fine_columns, aggregate.reshape(1, rows), coarse_columns],
        [
            pltpu.VMEM(fine_inv.shape, bf16),
            pltpu.VMEM(full, F32),
            pltpu.VMEM((slots, rows), i32),
            pltpu.VMEM((1, rows), i32),
            pltpu.VMEM(coarse_columns.shape, i32),
            sem((12,)),
        ],
        far=True,
    )
    rim_blocks, core_blocks = call(
        widen_kernel,
        [blocks, (blocks, bf16)],
        [fine_diag, fine_off],
        [pltpu.VMEM((slots + 1, size, size, rows), bf16), sem((slots + 1, 4))],
        far=True,
        limit=12,
    )
    ends = [jnp.transpose(coarse_diag, (0, 2, 1)), jnp.transpose(coarse_inv, (0, 2, 1))]
    cdiag, cinv = call(coarse_ends_kernel, [turned, turned], ends)
    others = jnp.transpose(coarse_off, (0, 1, 3, 2))
    coff = call(coarse_off_kernel, [(size, size, LANES)], [others])

    rim_work = [pltpu.VMEM((slots,) + half, F32), work[1]]
    ready = [half, (slots,) + half, (size, 8, LANES)]

    def core_args(rim, core):
        return [core_cols, core_blocks, core_rhs, rim, core, rim_cols, rim_blocks]

    def sweep_core(rim, core):
        return call(core_kernel, ready, core_args(rim, core) + [core_inv], work)

    def rim_args(rim, inside, lead, sent):
        return [rim_cols, rim_blocks, rim_inv, rim_rhs, rim, inside, lead, *sent]

    def sweep(rim, core):
        sent = exchange(rim, ways)
        core, inside, lead = sweep_core(rim, core)
        return call(rim_kernel, [half], rim_args(rim, inside, lead, sent), rim_work), core

    for cycle in range(CYCLES):
        for step in range(SWEEPS):
            if cycle:
                rim, core = sweep(rim, core)
            elif step:
                sent = exchange(rim, ways)
                inside, lead = call(lead_kernel, ready[1:], [rim, core, rim_cols, rim_blocks])
                args = [core_cols, core_blocks, core_rhs, rim, core, core_inv]
                new_core = call(core_alone_kernel, [half], args, work)
                rim = call(rim_kernel, [half], rim_args(rim, inside, lead, sent), rim_work)
                core = new_core
        sent = exchange(rim, ways)
        core_res, inside, lead = call(core_residual_kernel, ready, core_args(rim, core), work)
        crhs, u = call(
            restrict_kernel,
            [packed, packed],
            [rim_cols, rim_blocks, rim_rhs, core_res, inside, lead, *sent, core_cols, cinv],
            rim_work,
        )
        for step in range(1, CSWEEPS):
            base = [near, cdiag, coff, cinv, crhs, u, *exchange(u, ways)]
            if step < CSWEEPS - 1:
                u = call(coarse_kernel, [packed], base)
            else:
                rim, core = call(prolong_kernel, [half, half], base + [rim_cols, core_cols, rim, core])
        for step in range(SWEEPS - (cycle == CYCLES - 1)):
            rim, core = sweep(rim, core)
    sent = exchange(rim, ways)
    core, inside, lead = sweep_core(rim, core)
    args = rim_args(rim, inside, lead, sent) + [core]
    return pl.pallas_call(
        last_kernel,
        out_shape=pltpu.HBM(full, F32),
        in_specs=[VM] * len(args),
        out_specs=FAR,
        scratch_shapes=rim_work + [pltpu.VMEM(full, F32), sem((4, 2))],
        compiler_params=pltpu.CompilerParams(vmem_limit_bytes=4 * 1024 * 1024),
    )(*[in_vmem(a) for a in args])


def solution(mesh):
    placed = (
        P(None, AXES),
        P(None, None, AXES),
        P(None, None, None, AXES),
        P(None, None, AXES),
        P(None, AXES),
        P(AXES),
        P(None, None, AXES),
        P(None, None, None, AXES),
        P(None, None, AXES),
        P(None, AXES),
    )
    return jax.shard_map(
        shards, mesh=mesh, in_specs=placed, out_specs=P(None, AXES), check_vma=False
    )
```
